512 devices in a mesh: hst: 16 (over z, x_hi), dev: 32 (over y, x_lo, core).
Axes of the slice: x: 4 (x_hi: 2, x_lo: 2; x = x_hi * 2 + x_lo), y: 8, z: 8, core: 2. Of those that a mesh axis runs over, the one named last changes fastest.
Arguments:
- ctx_query: bfloat16 [8192, 8192], P('hst', 'dev'), may hold values from -8 to 8
- ctx_key: bfloat16 [8192, 1024], P(('hst', 'dev')), may hold values from -8 to 8
- ctx_value: bfloat16 [8192, 1024], P(('hst', 'dev')), may hold values from -6 to 6
- query: bfloat16 [1024, 8192], P('hst', 'dev'), may hold values from -8 to 8
- block_lengths: int32 [16], replicated, may hold values from 2 to 512, as said below
- query_positions: int32 [1024], replicated, may hold values from 2 to 8192, as said below
Outputs:
- ctx_out: bfloat16 [8192, 8192], P('hst', 'dev')
- query_out: bfloat16 [1024, 8192], P('hst', 'dev')
The draws below stay inside these ranges and needn't reach their ends.
Inputs may be any that keep to these rules, and one draw needn't show every extreme that they name: `block_lengths`: the first host block is full, of length 512. `query_positions`: some query token sees the whole context.
All inputs are finite; a program needn't handle non-finite values.
Results may differ from the reference program's by a relative error of at most 0.0039.
Values may be sent and summed in bfloat16 or wider, within the bound.
No kernel may reach another device: no remote copies, remote signals or barrier semaphores. Data moves between devices by JAX's collectives and lax.ppermute only.
A program may use at most 64 MiB of HBM per device.

```python
import math
import jax
import jax.numpy as jnp
from jax import lax

H = 64
KVH = 8
HD = 128
BLK_DEV = 16
QN_DEV = 64
CONTEXT = 8192
N_HST = 16
N_DEV = 32


def sign_table(key):
    picks = jax.random.bernoulli(jax.random.fold_in(key, 71), 0.5, (N_HST, KVH, HD))
    return jnp.where(picks, 1.0, -1.0).astype(jnp.float32)


def base_values(key, shape, width):
    return jnp.clip(jax.random.normal(key, shape, jnp.float32), -width, width)


def draw_ctx_key(key, part):
    signs = sign_table(key)
    key = jax.random.fold_in(key, 11)
    block_rows = BLK_DEV * N_DEV
    shape = (N_HST, block_rows, KVH * HD)
    base = base_values(key, shape, 6.0)
    first_row = 8.0 * signs
    trimmed = jnp.arange(HD) < max(HD // 8, 1)
    second_row = first_row - jnp.where(trimmed, 3.0 / math.sqrt(HD) * signs, 0.0)
    base = base.at[:, 0].set(first_row.reshape(N_HST, KVH * HD))
    base = base.at[:, 1].set(second_row.reshape(N_HST, KVH * HD))
    return base.reshape(N_HST * block_rows, KVH * HD).astype(jnp.bfloat16)


def draw_ctx_query(key, part):
    signs = sign_table(key)
    key = jax.random.fold_in(key, 13)
    base_key, mask_key, level_key = jax.random.split(key, 3)
    block_rows = BLK_DEV * N_DEV
    group_size = H // KVH
    shape = (N_HST, block_rows, H, HD)
    base = base_values(base_key, shape, 6.0)
    offsets = jnp.arange(block_rows)
    chosen = jax.random.bernoulli(mask_key, 1.0 / 16, (N_HST, block_rows, H)) & (offsets >= 1)[None, :, None]
    levels = jnp.array([3.0, 5.0, 8.0], jnp.float32)[jax.random.randint(level_key, (N_HST, block_rows, H), 0, 3)]
    head_signs = jnp.repeat(signs, group_size, axis=1)
    aligned = levels[..., None] * head_signs[:, None]
    base = jnp.where(chosen[..., None], aligned, base)
    return base.reshape(N_HST * block_rows, H * HD).astype(jnp.bfloat16)


def draw_query(key, part):
    signs = sign_table(key)
    key = jax.random.fold_in(key, 17)
    base_key, mask_key, level_key, block_key = jax.random.split(key, 4)
    count = QN_DEV * N_HST
    group_size = H // KVH
    shape = (count, H, HD)
    base = base_values(base_key, shape, 6.0)
    chosen = jax.random.bernoulli(mask_key, 1.0 / 8, (count, H))
    levels = jnp.array([3.0, 5.0, 8.0], jnp.float32)[jax.random.randint(level_key, (count, H), 0, 3)]
    target_block = jax.random.randint(block_key, (count, H), 0, N_HST)
    head_signs = jnp.repeat(signs, group_size, axis=1)
    picked = head_signs[target_block, jnp.arange(H)[None, :]]
    aligned = levels[..., None] * picked
    base = jnp.where(chosen[..., None], aligned, base)
    return base.reshape(count, H * HD).astype(jnp.bfloat16)


def draw_block_lengths(key, part):
    key = jax.random.fold_in(key, 5)
    block_rows = BLK_DEV * N_DEV
    lengths = jax.random.randint(key, (N_HST,), 2, block_rows + 1)
    return jnp.where(jnp.arange(N_HST) == 0, block_rows, lengths).astype(jnp.int32)


def draw_query_positions(key, part):
    key = jax.random.fold_in(key, 9)
    first, second = jax.random.split(key)
    count = QN_DEV * N_HST
    context = BLK_DEV * N_DEV * N_HST
    positions = jax.random.randint(first, (count,), 2, context + 1)
    chosen = jax.random.randint(second, (), 0, count)
    return jnp.where(jnp.arange(count) == chosen, context, positions).astype(jnp.int32)


def steps_of(stream_key, extent, cuts, low, largest):
    factor_of, own = 1.0, jax.random.fold_in(stream_key, 6)
    for dim, blocks in cuts:
        draws = jnp.exp(jax.random.uniform(jax.random.fold_in(own, dim), (blocks,), jnp.float32, low / len(cuts), largest / len(cuts)))
        factor_of = factor_of * jnp.repeat(draws, extent[dim] // blocks).reshape([-1 if axis == dim else 1 for axis in range(len(extent))])
    return factor_of


def gaussian(rng, extent, spread, limit, cuts=(), kind=jnp.bfloat16):
    gain = steps_of(rng, extent, cuts, -0.22, 0.18) if cuts else 1.0
    drawn = jax.random.normal(rng, extent, jnp.float32) * spread * gain
    return jnp.minimum(jnp.maximum(drawn, -limit), limit).astype(kind)


def setup_inputs(seed: int = 0) -> dict:
    key_of = jax.random.split(jax.random.key(seed), 7)
    ctx_query = draw_ctx_query(jax.random.fold_in(key_of[6], 71), 0)
    ctx_key = draw_ctx_key(jax.random.fold_in(key_of[6], 71), 0)
    ctx_value = gaussian(key_of[2], (CONTEXT, KVH * HD), 1.0, 6.0, ((0, 512),))
    query = draw_query(jax.random.fold_in(key_of[6], 71), 0)
    block_lengths = draw_block_lengths(jax.random.fold_in(key_of[6], 71), 0)
    query_positions = draw_query_positions(jax.random.fold_in(key_of[6], 71), 0)
    return {"ctx_query": ctx_query, "ctx_key": ctx_key, "ctx_value": ctx_value, "query": query, "block_lengths": block_lengths, "query_positions": query_positions}


NEG = -1e30


def softmax_attend(queries, keys, values, visible):
    scores = jnp.dot(queries, keys.T, preferred_element_type=jnp.float32) * (HD ** -0.5)
    scores = jnp.where(visible, scores, NEG)
    maxima = jnp.max(scores, axis=-1, keepdims=True)
    weights = jnp.where(visible, jnp.exp(scores - maxima), 0.0)
    totals = jnp.sum(weights, axis=-1, keepdims=True)
    mixed = jnp.dot(weights.astype(jnp.bfloat16), values, preferred_element_type=jnp.float32)
    return mixed / totals


def reference(ctx_query, ctx_key, ctx_value, query, block_lengths, query_positions):
    block_rows = BLK_DEV * N_DEV
    group_size = H // KVH
    all_queries = ctx_query.reshape(N_HST, block_rows, H, HD)
    all_keys = ctx_key.reshape(N_HST, block_rows, KVH, HD)
    all_values = ctx_value.reshape(N_HST, block_rows, KVH, HD)
    row_ids = jnp.arange(block_rows, dtype=jnp.int32)

    def one_host(host_index):
        keys = jnp.concatenate([all_keys[0], all_keys[host_index]], axis=0)
        values = jnp.concatenate([all_values[0], all_values[host_index]], axis=0)
        anchor_seen = (row_ids < block_lengths[0]) & (host_index > 0)
        anchor_mask = jnp.broadcast_to(anchor_seen[None, :], (block_rows, block_rows))
        local_mask = (row_ids[None, :] <= row_ids[:, None]) & (row_ids[None, :] < block_lengths[host_index])
        visible = jnp.concatenate([anchor_mask, local_mask], axis=1)
        host_queries = all_queries[host_index]

        def one_head(head):
            return softmax_attend(host_queries[:, head], keys[:, head // group_size], values[:, head // group_size], visible)

        mixed = lax.map(one_head, jnp.arange(H, dtype=jnp.int32))
        return jnp.transpose(mixed, (1, 0, 2)).reshape(block_rows, H * HD)

    ctx_out = lax.map(one_host, jnp.arange(N_HST, dtype=jnp.int32))
    ctx_out = ctx_out.reshape(N_HST * block_rows, H * HD).astype(jnp.bfloat16)

    count = QN_DEV * N_HST
    positions = jnp.arange(N_HST * block_rows, dtype=jnp.int32)
    live = (positions % block_rows) < block_lengths[positions // block_rows]
    visible = live[None, :] & (positions[None, :] < query_positions[:, None])
    query_heads = query.reshape(count, H, HD)
    flat_keys = ctx_key.reshape(N_HST * block_rows, KVH, HD)
    flat_values = ctx_value.reshape(N_HST * block_rows, KVH, HD)

    def query_head(head):
        return softmax_attend(query_heads[:, head], flat_keys[:, head // group_size], flat_values[:, head // group_size], visible)

    mixed = lax.map(query_head, jnp.arange(H, dtype=jnp.int32))
    query_out = jnp.transpose(mixed, (1, 0, 2)).reshape(count, H * HD).astype(jnp.bfloat16)
    return ctx_out, query_out
```

```python
import math

import jax
import jax.numpy as jnp
from jax import lax
from jax.experimental import pallas as pl
from jax.experimental.pallas import tpu as pltpu
from jax.sharding import PartitionSpec as P

H = 64
KVH = 8
HD = 128
N_Z = 8
N_PAIR = 2
N_LANE = 4
BLK_DEV = 16
QN_DEV = 64
ROWS = 512
SHARE = KVH * BLK_DEV
STAT = 16

NEG = -1e30
FAR = 1 << 20
SCALE2 = HD ** (-0.5) * math.log2(math.e)
BF = jnp.bfloat16
F32 = jnp.float32
NT = (((1,), (1,)), ((), ()))
VMEM_LIMIT = 48 * 1024 * 1024


def call(kernel, out_shape, scratch=(), cost=0):
    return pl.pallas_call(
        kernel,
        out_shape=out_shape,
        scratch_shapes=list(scratch),
        compiler_params=pltpu.CompilerParams(vmem_limit_bytes=VMEM_LIMIT),
        cost_estimate=pl.CostEstimate(
            flops=cost, bytes_accessed=cost // 500, transcendentals=cost // 500
        ),
    )


def pack_kernel(key_ref, value_ref, out_ref):
    for head in range(KVH):
        cols = slice(head * HD, (head + 1) * HD)
        both = jnp.concatenate([key_ref[:, cols], value_ref[:, cols]], axis=1)
        for z in range(N_Z):
            out_ref[z * KVH + head] = both


def with_ones(values):
    return jnp.concatenate([values, jnp.ones_like(values)], axis=1)


def far_kernel(mine_ref, other_ref, kv_ref, pos_ref, len_ref, place_ref, out_ref, q_ref):
    z = place_ref[0]
    pair = place_ref[1]
    lane = place_ref[2]
    q_ref[pair] = mine_ref[...]
    q_ref[1 - pair] = other_ref[...]
    count = kv_ref.shape[0]
    n = lax.broadcasted_iota(jnp.int32, (1, count), 1)
    host = (n // SHARE) * N_PAIR + pair
    inner = ((n % SHARE) // BLK_DEV * N_LANE + lane) * BLK_DEV + n % BLK_DEV
    length = jnp.zeros((1, count), jnp.int32)
    for h in range(N_Z):
        length = jnp.where(n // SHARE == h, len_ref[h * N_PAIR + pair], length)
    spot = jnp.where(inner < length, host * ROWS + inner, FAR).astype(F32)
    limits = jnp.broadcast_to(pos_ref[pl.ds(z, 1), :].astype(F32), (HD, HD)).T
    keys = kv_ref[:, :HD]
    values = with_ones(kv_ref[:, HD:])
    for p in range(N_PAIR):
        lim = limits[p * QN_DEV:(p + 1) * QN_DEV]
        lim = jnp.concatenate([jnp.concatenate([lim] * 4, axis=0)] * (count // HD), axis=1)
        for g in range(0, N_LANE, 2):
            q = q_ref[p, g * QN_DEV:(g + 2) * QN_DEV, :]
            q = jnp.concatenate(
                [q[:QN_DEV, :HD], q[:QN_DEV, HD:], q[QN_DEV:, :HD], q[QN_DEV:, HD:]], axis=0
            )
            s = lax.dot_general(q, keys, NT, preferred_element_type=F32)
            s = jnp.where(spot < lim, s, NEG)
            top = jnp.max(s, axis=1, keepdims=True)
            w = jnp.exp2((s - top) * SCALE2).astype(BF)
            mixed = jnp.dot(w, values, preferred_element_type=F32)
            total = mixed[:, HD:]
            level = top * SCALE2 + jnp.log2(total)
            mean = (mixed[:, :HD] / total).astype(BF)
            for j in range(2):
                d = p * N_LANE + g + j
                base = j * 2 * QN_DEV
                out_ref[d, :QN_DEV, :HD] = mean[base:base + QN_DEV]
                out_ref[d, :QN_DEV, HD:] = mean[base + QN_DEV:base + 2 * QN_DEV]
                flat = level[base:base + 2 * QN_DEV].T[:STAT]
                high = flat.astype(BF)
                rest = flat - high.astype(F32)
                mid = rest.astype(BF)
                low = (rest - mid.astype(F32)).astype(BF)
                row = lax.broadcasted_iota(jnp.int32, (STAT, HD), 0)
                stat = jnp.where(
                    row == 0,
                    high.astype(F32),
                    jnp.where(row == 1, mid.astype(F32), low.astype(F32)),
                )
                out_ref[d, QN_DEV:, :HD] = stat.astype(BF)
                out_ref[d, QN_DEV:, HD:] = jnp.zeros((STAT, HD), BF)


def merge_kernel(in_ref, out_ref):
    parts = in_ref.shape[0]
    levels = []
    for k in range(parts):
        stat = in_ref[k, QN_DEV:, :HD].astype(F32)
        levels.append(stat[0:1] + stat[1:2] + stat[2:3])
    level = jnp.concatenate(levels, axis=0)
    w = jnp.exp2(level - jnp.max(level, axis=0, keepdims=True))
    w = w / jnp.sum(w, axis=0, keepdims=True)
    w = jnp.concatenate([w, jnp.zeros((HD - parts, HD), F32)], axis=0).T
    for h in range(2):
        mixed = jnp.zeros((QN_DEV, HD), F32)
        for k in range(parts):
            column = w[h * QN_DEV:(h + 1) * QN_DEV, k:k + 1]
            mixed += column * in_ref[k, :QN_DEV, h * HD:(h + 1) * HD].astype(F32)
        out_ref[:, h * HD:(h + 1) * HD] = mixed.astype(BF)


def ctx_kernel(q_ref, kv_ref, len_ref, place_ref, out_ref, local_ref):
    host = place_ref[0] * N_PAIR + place_ref[1]
    own = len_ref[host]
    bias = jnp.where(host == 0, jnp.float32(NEG), jnp.float32(0.0))
    for y in range(KVH):
        for g in range(N_LANE):
            to = (y * N_LANE + g) * BLK_DEV
            at = g * 2 * SHARE + y * BLK_DEV
            local_ref[to:to + BLK_DEV, :] = kv_ref[at:at + BLK_DEV, :]
    anchor = jnp.concatenate(
        [kv_ref[g * 2 * SHARE + SHARE:(g + 1) * 2 * SHARE, :] for g in range(N_LANE)], axis=0
    )
    anchor_key, anchor_value = anchor[:, :HD], with_ones(anchor[:, HD:])
    step = 128
    for i in range(ROWS // step):
        n = (i + 1) * step
        rows = slice(i * step, n)
        q = jnp.concatenate([q_ref[rows, :HD], q_ref[rows, HD:]], axis=0)
        a = lax.dot_general(q, anchor_key, NT, preferred_element_type=F32) + bias
        b = lax.dot_general(q, local_ref[:n, :HD], NT, preferred_element_type=F32)
        col = lax.broadcasted_iota(jnp.int32, (2 * step, n), 1)
        row = lax.broadcasted_iota(jnp.int32, (2 * step, n), 0) % step + i * step
        b = jnp.where((col <= row) & (col < own), b, NEG)
        top = jnp.maximum(
            jnp.max(a, axis=1, keepdims=True), jnp.max(b, axis=1, keepdims=True)
        )
        a = jnp.exp2((a - top) * SCALE2).astype(BF)
        b = jnp.exp2((b - top) * SCALE2).astype(BF)
        mixed = jnp.dot(a, anchor_value, preferred_element_type=F32)
        mixed += jnp.dot(b, with_ones(local_ref[:n, HD:]), preferred_element_type=F32)
        mean = (mixed[:, :HD] / mixed[:, HD:]).astype(BF)
        out_ref[rows, :HD] = mean[:step]
        out_ref[rows, HD:] = mean[step:]


def groups(mesh):
    z, x, y, g = range(N_Z), range(N_PAIR), range(KVH), range(N_LANE)
    at = lambda c, d, e, f: (c * N_PAIR + d) * KVH * N_LANE + e * N_LANE + f
    plane = [[at(c, d, e, f) for c in z for e in y] for d in x for f in g]
    line = [[at(c, d, e, f) for d in x for f in g] for c in z for e in y]
    four = [[e * N_LANE + f for f in g] for e in y]
    return plane, line, four


def solution(mesh):
    plane, line, four = groups(mesh)
    both = ("hst", "dev")

    def per_device(ctx_query, ctx_key, ctx_value, query, block_lengths, query_positions):
        host = lax.axis_index("hst")
        z, pair = host // N_PAIR, host % N_PAIR
        place = jnp.stack([z, pair, lax.axis_index("dev") % N_LANE])

        mine = lax.all_gather(query, "dev", axis=0, tiled=True, axis_index_groups=four)
        other = lax.ppermute(mine, "hst", [(i, i ^ 1) for i in range(N_Z * N_PAIR)])

        send = call(pack_kernel, jax.ShapeDtypeStruct((N_Z * KVH, BLK_DEV, 2 * HD), BF))(
            ctx_key, ctx_value
        )
        share = lax.all_to_all(send, both, 0, 0, axis_index_groups=plane)
        share = share.reshape(N_Z * SHARE, 2 * HD)

        first = share[:SHARE]
        passed = lax.ppermute(first, "hst", [(2 * i, 2 * i + 1) for i in range(N_Z)])
        anchor = jnp.where(pair == 0, first, passed)
        local = lax.dynamic_slice_in_dim(share, z * SHARE, SHARE, 0)
        near = lax.all_gather(
            jnp.concatenate([local, anchor], axis=0),
            "dev", axis=0, tiled=True, axis_index_groups=four,
        )

        smem = pl.BlockSpec(memory_space=pltpu.SMEM)
        vmem = pl.BlockSpec(memory_space=pltpu.VMEM)
        params = pltpu.CompilerParams(vmem_limit_bytes=VMEM_LIMIT)
        dests = N_PAIR * N_LANE
        partial = pl.pallas_call(
            far_kernel,
            out_shape=jax.ShapeDtypeStruct((dests, QN_DEV + STAT, 2 * HD), BF),
            in_specs=[vmem, vmem, vmem, vmem, smem, smem],
            out_specs=vmem,
            scratch_shapes=[pltpu.VMEM((N_PAIR, N_LANE * QN_DEV, 2 * HD), BF)],
            compiler_params=params,
            cost_estimate=pl.CostEstimate(
                flops=800_000_000, bytes_accessed=1_200_000, transcendentals=1 << 20
            ),
        )(mine, other, share, query_positions.reshape(N_Z, N_PAIR * QN_DEV), block_lengths, place)
        arrived = lax.all_to_all(partial, both, 0, 0, axis_index_groups=line)

        ctx_out = pl.pallas_call(
            ctx_kernel,
            out_shape=jax.ShapeDtypeStruct(ctx_query.shape, BF),
            in_specs=[vmem, vmem, smem, smem],
            out_specs=vmem,
            scratch_shapes=[pltpu.VMEM((ROWS, 2 * HD), BF)],
            compiler_params=params,
            cost_estimate=pl.CostEstimate(
                flops=800_000_000, bytes_accessed=1_200_000, transcendentals=1 << 20
            ),
        )(ctx_query, near, block_lengths, place)
        query_out = call(merge_kernel, jax.ShapeDtypeStruct(query.shape, BF))(arrived)
        return ctx_out, query_out

    return jax.shard_map(
        per_device,
        mesh=mesh,
        in_specs=(
            P("hst", "dev"),
            P(("hst", "dev"), None),
            P(("hst", "dev"), None),
            P("hst", "dev"),
            P(),
            P(),
        ),
        out_specs=(P("hst", "dev"), P("hst", "dev")),
        check_vma=False,
    )
```

```python
import math

import jax
import jax.numpy as jnp
from jax import lax
from jax.experimental import pallas as pl
from jax.experimental.pallas import tpu as pltpu
from jax.sharding import PartitionSpec as P

H = 64
KVH = 8
HD = 128
N_Z = 8
N_PAIR = 2
N_LANE = 4
BLK_DEV = 16
QN_DEV = 64
ROWS = 512
SHARE = KVH * BLK_DEV
STAT = 16

FAR_ROWS = 256
CTX_ROWS = 128
NEG = -1e30
FAR = 1 << 20
SCALE2 = HD ** (-0.5) * math.log2(math.e)
BF = jnp.bfloat16
F32 = jnp.float32
NT = (((1,), (1,)), ((), ()))
VMEM_LIMIT = 48 * 1024 * 1024


def pack_kernel(key_hbm, value_hbm, out_hbm, key_ref, value_ref, out_ref, sems):
    fetch = [
        pltpu.make_async_copy(key_hbm, key_ref, sems.at[0]),
        pltpu.make_async_copy(value_hbm, value_ref, sems.at[1]),
    ]
    for copy in fetch:
        copy.start()
    for copy in fetch:
        copy.wait()
    for head in range(KVH):
        cols = slice(head * HD, (head + 1) * HD)
        out_ref[head] = jnp.concatenate([key_ref[:, cols], value_ref[:, cols]], axis=1)
    store = [
        pltpu.make_async_copy(out_ref, out_hbm.at[pl.ds(z * KVH, KVH)], sems.at[2 + z])
        for z in range(N_Z)
    ]
    for copy in store:
        copy.start()
    for copy in store:
        copy.wait()


def with_ones(values):
    return jnp.concatenate([values, jnp.ones_like(values)], axis=1)


def prep_kernel(seen_ref, pos_ref, len_ref, place_ref, q_ref, spot_ref, lim_ref, info_ref):
    z = place_ref[0]
    pair = place_ref[1]
    lane = place_ref[2]
    info_ref[0] = z * N_PAIR + pair
    info_ref[1] = len_ref[z * N_PAIR + pair]
    for g in range(N_LANE):
        for p in range(N_PAIR):
            at = (g * N_PAIR + p) * QN_DEV
            for h in range(2):
                rows = slice((2 * g + h) * QN_DEV, (2 * g + h + 1) * QN_DEV)
                q_ref[p, rows] = seen_ref[at:at + QN_DEV, h * HD:(h + 1) * HD]
    n = lax.broadcasted_iota(jnp.int32, spot_ref.shape, 1)
    host = (n // SHARE) * N_PAIR + pair
    inner = ((n % SHARE) // BLK_DEV * N_LANE + lane) * BLK_DEV + n % BLK_DEV
    length = jnp.zeros(spot_ref.shape, jnp.int32)
    for h in range(N_Z):
        length = jnp.where(n // SHARE == h, len_ref[h * N_PAIR + pair], length)
    spot_ref[...] = jnp.where(inner < length, host * ROWS + inner, FAR).astype(F32)
    lim_ref[...] = jnp.broadcast_to(pos_ref[pl.ds(z, 1), :].astype(F32), (HD, HD)).T


def far_kernel(q_ref, kv_ref, spot_ref, lim_ref, out_hbm, out_ref, sems):
    count = kv_ref.shape[0]
    spot = spot_ref[0:1, :]
    keys = kv_ref[:, :HD]
    values = with_ones(kv_ref[:, HD:])
    per = FAR_ROWS // QN_DEV
    blocks = [(p, r) for p in range(N_PAIR) for r in range(0, 2 * N_LANE * QN_DEV, FAR_ROWS)]
    stores = []

    def score(block):
        p, r = block
        return lax.dot_general(
            q_ref[p, r:r + FAR_ROWS], keys, NT, preferred_element_type=F32
        )

    def finish(block, s):
        p, r = block
        lim = lim_ref[p * QN_DEV:(p + 1) * QN_DEV, :]
        lim = jnp.concatenate([jnp.concatenate([lim] * per, axis=0)] * (count // HD), axis=1)
        s = jnp.where(spot < lim, s, NEG)
        top = jnp.max(s, axis=1, keepdims=True)
        w = jnp.exp2((s - top) * SCALE2).astype(BF)
        mixed = jnp.dot(w, values, preferred_element_type=F32)
        total = mixed[:, HD:]
        level = top * SCALE2 + jnp.log2(total)
        mean = (mixed[:, :HD] / total).astype(BF)
        first = p * N_LANE + r // (2 * QN_DEV)
        for j in range(per // 2):
            d = first + j
            base = j * 2 * QN_DEV
            out_ref[d, :QN_DEV, :HD] = mean[base:base + QN_DEV]
            out_ref[d, :QN_DEV, HD:] = mean[base + QN_DEV:base + 2 * QN_DEV]
            flat = level[base:base + 2 * QN_DEV].T[:STAT]
            high = flat.astype(BF).astype(F32)
            rest = flat - high
            mid = rest.astype(BF).astype(F32)
            row = lax.broadcasted_iota(jnp.int32, (STAT, HD), 0)
            stat = jnp.where(row == 0, high, jnp.where(row == 1, mid, rest - mid))
            out_ref[d, QN_DEV:, :HD] = stat.astype(BF)
            out_ref[d, QN_DEV:, HD:] = jnp.zeros((STAT, HD), BF)
        part = pl.ds(first, per // 2)
        copy = pltpu.make_async_copy(out_ref.at[part], out_hbm.at[part], sems.at[len(stores)])
        copy.start()
        stores.append(copy)

    ahead = score(blocks[0])
    for k, block in enumerate(blocks):
        s = ahead
        if k + 1 < len(blocks):
            ahead = score(blocks[k + 1])
        finish(block, s)
    for copy in stores:
        copy.wait()


def merge_kernel(in_ref, out_ref):
    parts = in_ref.shape[0]
    levels = []
    for k in range(parts):
        stat = in_ref[k, QN_DEV:, :HD].astype(F32)
        levels.append(stat[0:1] + stat[1:2] + stat[2:3])
    level = jnp.concatenate(levels, axis=0)
    w = jnp.exp2(level - jnp.max(level, axis=0, keepdims=True))
    w = w / jnp.sum(w, axis=0, keepdims=True)
    w = jnp.concatenate([w, jnp.zeros((HD - parts, HD), F32)], axis=0).T
    for h in range(2):
        mixed = jnp.zeros((QN_DEV, HD), F32)
        for k in range(parts):
            column = w[h * QN_DEV:(h + 1) * QN_DEV, k:k + 1]
            mixed += column * in_ref[k, :QN_DEV, h * HD:(h + 1) * HD].astype(F32)
        out_ref[:, h * HD:(h + 1) * HD] = mixed.astype(BF)


def ctx_kernel(q_ref, kv_ref, info_ref, ctx_hbm, ctx_ref, local_ref, sems):
    alone = info_ref[0] == 0
    own = info_ref[1]
    stores = []
    for y in range(KVH):
        for g in range(N_LANE):
            to = (y * N_LANE + g) * BLK_DEV
            at = (g % 2 * 4 + g // 2) * SHARE + y * BLK_DEV
            local_ref[to:to + BLK_DEV, :] = kv_ref[at:at + BLK_DEV, :]
    anchor = jnp.concatenate(
        [kv_ref[(4 * c + 2) * SHARE:(4 * c + 4) * SHARE, :] for c in range(2)], axis=0
    )
    anchor_key, anchor_value = anchor[:, :HD], with_ones(anchor[:, HD:])
    step = CTX_ROWS
    col = lax.broadcasted_iota(jnp.int32, (1, ROWS), 1)
    spot = jnp.where(col < own, col, FAR)

    def score(i):
        rows = slice(i * step, (i + 1) * step)
        q = jnp.concatenate([q_ref[rows, :HD], q_ref[rows, HD:]], axis=0)
        a = lax.dot_general(q, anchor_key, NT, preferred_element_type=F32)
        b = lax.dot_general(q, local_ref[:(i + 1) * step, :HD], NT, preferred_element_type=F32)
        return a, b

    def finish(i, a, b):
        n = (i + 1) * step
        rows = slice(i * step, n)
        row = lax.broadcasted_iota(jnp.int32, (2 * step, n), 0) % step + i * step
        b = jnp.where(spot[:, :n] <= row, b, NEG)
        top_a = jnp.max(a, axis=1, keepdims=True)
        top = jnp.maximum(jnp.where(alone, NEG, top_a), jnp.max(b, axis=1, keepdims=True))
        a = jnp.exp2((a - jnp.where(alone, -NEG, top)) * SCALE2).astype(BF)
        b = jnp.exp2((b - top) * SCALE2).astype(BF)
        mixed = jnp.dot(a, anchor_value, preferred_element_type=F32)
        mixed += jnp.dot(b, with_ones(local_ref[:n, HD:]), preferred_element_type=F32)
        mean = (mixed[:, :HD] / mixed[:, HD:]).astype(BF)
        ctx_ref[rows, :HD] = mean[:step]
        ctx_ref[rows, HD:] = mean[step:]
        part = pl.ds(i * step, step)
        copy = pltpu.make_async_copy(ctx_ref.at[part], ctx_hbm.at[part], sems.at[i])
        copy.start()
        stores.append(copy)

    count = ROWS // step
    ahead = score(0)
    for i in range(count):
        a, b = ahead
        if i + 1 < count:
            ahead = score(i + 1)
        finish(i, a, b)
    for copy in stores:
        copy.wait()


def groups():
    z, x, y, g = range(N_Z), range(N_PAIR), range(KVH), range(N_LANE)
    at = lambda c, d, e, f: (c * N_PAIR + d) * KVH * N_LANE + e * N_LANE + f
    plane = [[at(c, d, e, f) for c in z for e in y] for d in x for f in g]
    line = [[at(c, d, e, f) for d in x for f in g] for c in z for e in y]
    four = [[e * N_LANE + f for f in g] for e in y]
    side = [[at(c, d, e, 2 * f + k) for d in x for f in range(2)] for c in z for e in y for k in range(2)]
    chip = [[2 * f, 2 * f + 1] for f in range(KVH * N_LANE // 2)]
    pairs = [[2 * c, 2 * c + 1] for c in z]
    return plane, line, four, side, chip, pairs


def solution(mesh):
    plane, line, four, side, chip, pairs = groups()
    both = ("hst", "dev")

    def per_device(ctx_query, ctx_key, ctx_value, query, block_lengths, query_positions):
        host = lax.axis_index("hst")
        z, pair = host // N_PAIR, host % N_PAIR
        smem = pl.BlockSpec(memory_space=pltpu.SMEM)
        vmem = pl.BlockSpec(memory_space=pltpu.VMEM)
        hbm = pl.BlockSpec(memory_space=pltpu.HBM)
        params = pltpu.CompilerParams(vmem_limit_bytes=VMEM_LIMIT)
        heavy = pl.CostEstimate(
            flops=800_000_000, bytes_accessed=1_200_000, transcendentals=1 << 20
        )
        dma = pltpu.SemaphoreType.DMA
        shape = lambda dims, dtype: jax.ShapeDtypeStruct(dims, dtype)

        send = pl.pallas_call(
            pack_kernel,
            out_shape=shape((N_Z * KVH, BLK_DEV, 2 * HD), BF),
            in_specs=[hbm, hbm],
            out_specs=hbm,
            scratch_shapes=[
                pltpu.VMEM(ctx_key.shape, BF),
                pltpu.VMEM(ctx_value.shape, BF),
                pltpu.VMEM((KVH, BLK_DEV, 2 * HD), BF),
                dma((2 + N_Z,)),
            ],
        )(ctx_key, ctx_value)
        share = lax.all_to_all(send, both, 0, 0, axis_index_groups=plane)
        share = share.reshape(N_Z * SHARE, 2 * HD)

        couple = lax.all_gather(query, "hst", axis=0, tiled=True, axis_index_groups=pairs)
        seen = lax.all_gather(couple, "dev", axis=0, tiled=True, axis_index_groups=four)
        place = jnp.stack([z, pair, lax.axis_index("dev") % N_LANE, jnp.zeros_like(z)])
        spans = N_PAIR * QN_DEV
        ask, spot, limits, info = pl.pallas_call(
            prep_kernel,
            out_shape=(
                shape((N_PAIR, 2 * N_LANE * QN_DEV, HD), BF),
                shape((8, N_Z * SHARE), F32),
                shape((spans, spans), F32),
                shape((2,), jnp.int32),
            ),
            in_specs=[vmem, vmem, smem, smem],
            out_specs=(vmem, vmem, vmem, smem),
            compiler_params=params,
        )(seen, query_positions.reshape(N_Z, spans), block_lengths, place)

        share, ask, spot, limits, info = lax.optimization_barrier(
            (share, ask, spot, limits, info)
        )
        local = lax.dynamic_slice_in_dim(share, z * SHARE, SHARE, 0)
        mine = jnp.concatenate([local, share[:SHARE]], axis=0)
        beside = lax.all_to_all(
            jnp.broadcast_to(mine[None], (4, *mine.shape)), both, 0, 0, axis_index_groups=side
        )

        dests = N_PAIR * N_LANE
        piece = (dests, QN_DEV + STAT, 2 * HD)
        partial = pl.pallas_call(
            far_kernel,
            out_shape=shape(piece, BF),
            in_specs=[vmem, vmem, vmem, vmem],
            out_specs=hbm,
            scratch_shapes=[pltpu.VMEM(piece, BF), dma((dests,))],
            compiler_params=params,
            cost_estimate=heavy,
        )(ask, share, spot, limits)
        partial, beside = lax.optimization_barrier((partial, beside))
        half = beside.reshape(N_PAIR, 2, 2 * SHARE, 2 * HD)
        local = lax.dynamic_index_in_dim(half, pair, 0, keepdims=False)[:, :SHARE]
        near = lax.all_gather(
            jnp.stack([local, half[0, :, SHARE:]]).reshape(4 * SHARE, 2 * HD),
            "dev", axis=0, tiled=True, axis_index_groups=chip,
        )
        arrived = lax.all_to_all(partial, both, 0, 0, axis_index_groups=line)

        ctx_out = pl.pallas_call(
            ctx_kernel,
            out_shape=shape(ctx_query.shape, BF),
            in_specs=[vmem, vmem, smem],
            out_specs=hbm,
            scratch_shapes=[
                pltpu.VMEM(ctx_query.shape, BF),
                pltpu.VMEM((ROWS, 2 * HD), BF),
                dma((ROWS // CTX_ROWS,)),
            ],
            compiler_params=params,
            cost_estimate=heavy,
        )(ctx_query, near, info)
        query_out = pl.pallas_call(
            merge_kernel,
            out_shape=shape(query.shape, BF),
            in_specs=[vmem],
            out_specs=vmem,
            compiler_params=params,
        )(arrived)
        return ctx_out, query_out

    return jax.shard_map(
        per_device,
        mesh=mesh,
        in_specs=(
            P("hst", "dev"),
            P(("hst", "dev"), None),
            P(("hst", "dev"), None),
            P("hst", "dev"),
            P(),
            P(),
        ),
        out_specs=(P("hst", "dev"), P("hst", "dev")),
        check_vma=False,
    )
```

```python
import math

import jax
import jax.numpy as jnp
from jax import lax
from jax.experimental import pallas as pl
from jax.experimental.pallas import tpu as pltpu
from jax.sharding import PartitionSpec as P

H = 64
KVH = 8
HD = 128
N_Z = 8
N_PAIR = 2
N_LANE = 4
BLK_DEV = 16
QN_DEV = 64
ROWS = 512
SHARE = KVH * BLK_DEV
STAT = 16

FAR_ROWS = 256
CTX_ROWS = 128
NEG = -1e30
FAR = 1 << 20
SCALE2 = HD ** (-0.5) * math.log2(math.e)
BF = jnp.bfloat16
F32 = jnp.float32
NT = (((1,), (1,)), ((), ()))
VMEM_LIMIT = 48 * 1024 * 1024


def pack_kernel(key_hbm, value_hbm, out_hbm, key_ref, value_ref, out_ref, sems):
    fetch = [
        pltpu.make_async_copy(key_hbm, key_ref, sems.at[0]),
        pltpu.make_async_copy(value_hbm, value_ref, sems.at[1]),
    ]
    for copy in fetch:
        copy.start()
    for copy in fetch:
        copy.wait()
    for head in range(KVH):
        cols = slice(head * HD, (head + 1) * HD)
        out_ref[head] = jnp.concatenate([key_ref[:, cols], value_ref[:, cols]], axis=1)
    store = [
        pltpu.make_async_copy(out_ref, out_hbm.at[pl.ds(z * KVH, KVH)], sems.at[2 + z])
        for z in range(N_Z)
    ]
    for copy in store:
        copy.start()
    for copy in store:
        copy.wait()


def with_ones(values):
    return jnp.concatenate([values, jnp.ones_like(values)], axis=1)


def prep_kernel(seen_ref, pos_ref, len_ref, place_ref, q_ref, spot_ref, lim_ref, info_ref):
    z = place_ref[0]
    pair = place_ref[1]
    lane = place_ref[2]
    info_ref[0] = z * N_PAIR + pair
    info_ref[1] = len_ref[z * N_PAIR + pair]
    info_ref[2] = lane // 2
    for g in range(N_LANE):
        for p in range(N_PAIR):
            at = (g * N_PAIR + p) * QN_DEV
            for h in range(2):
                rows = slice((2 * g + h) * QN_DEV, (2 * g + h + 1) * QN_DEV)
                q_ref[p, rows] = seen_ref[at:at + QN_DEV, h * HD:(h + 1) * HD]
    n = lax.broadcasted_iota(jnp.int32, spot_ref.shape, 1)
    host = (n // SHARE) * N_PAIR + pair
    inner = ((n % SHARE) // BLK_DEV * N_LANE + lane) * BLK_DEV + n % BLK_DEV
    length = jnp.zeros(spot_ref.shape, jnp.int32)
    for h in range(N_Z):
        length = jnp.where(n // SHARE == h, len_ref[h * N_PAIR + pair], length)
    spot_ref[...] = jnp.where(inner < length, host * ROWS + inner, FAR).astype(F32)
    lim_ref[...] = jnp.broadcast_to(pos_ref[pl.ds(z, 1), :].astype(F32), (HD, HD)).T


def far_kernel(q_ref, kv_ref, spot_ref, lim_ref, out_hbm, out_ref, sems):
    count = kv_ref.shape[0]
    spot = spot_ref[0:1, :]
    keys = kv_ref[:, :HD]
    values = with_ones(kv_ref[:, HD:])
    per = FAR_ROWS // QN_DEV
    blocks = [(p, r) for p in range(N_PAIR) for r in range(0, 2 * N_LANE * QN_DEV, FAR_ROWS)]
    stores = []

    def score(block):
        p, r = block
        return lax.dot_general(
            q_ref[p, r:r + FAR_ROWS], keys, NT, preferred_element_type=F32
        )

    def finish(block, s):
        p, r = block
        lim = lim_ref[p * QN_DEV:(p + 1) * QN_DEV, :]
        lim = jnp.concatenate([jnp.concatenate([lim] * per, axis=0)] * (count // HD), axis=1)
        s = jnp.where(spot < lim, s, NEG)
        top = jnp.max(s, axis=1, keepdims=True)
        w = jnp.exp2((s - top) * SCALE2).astype(BF)
        mixed = jnp.dot(w, values, preferred_element_type=F32)
        total = mixed[:, HD:]
        level = top * SCALE2 + jnp.log2(total)
        mean = (mixed[:, :HD] / total).astype(BF)
        first = p * N_LANE + r // (2 * QN_DEV)
        for j in range(per // 2):
            d = first + j
            base = j * 2 * QN_DEV
            out_ref[d, :QN_DEV, :HD] = mean[base:base + QN_DEV]
            out_ref[d, :QN_DEV, HD:] = mean[base + QN_DEV:base + 2 * QN_DEV]
            flat = level[base:base + 2 * QN_DEV].T[:STAT]
            high = flat.astype(BF).astype(F32)
            rest = flat - high
            mid = rest.astype(BF).astype(F32)
            row = lax.broadcasted_iota(jnp.int32, (STAT, HD), 0)
            stat = jnp.where(row == 0, high, jnp.where(row == 1, mid, rest - mid))
            out_ref[d, QN_DEV:, :HD] = stat.astype(BF)
            out_ref[d, QN_DEV:, HD:] = jnp.zeros((STAT, HD), BF)
        part = pl.ds(first, per // 2)
        copy = pltpu.make_async_copy(out_ref.at[part], out_hbm.at[part], sems.at[len(stores)])
        copy.start()
        stores.append(copy)

    ahead = score(blocks[0])
    for k, block in enumerate(blocks):
        s = ahead
        if k + 1 < len(blocks):
            ahead = score(blocks[k + 1])
        finish(block, s)
    for copy in stores:
        copy.wait()


def merge_kernel(in_ref, out_ref):
    parts = in_ref.shape[0]
    levels = []
    for k in range(parts):
        stat = in_ref[k, QN_DEV:, :HD].astype(F32)
        levels.append(stat[0:1] + stat[1:2] + stat[2:3])
    level = jnp.concatenate(levels, axis=0)
    w = jnp.exp2(level - jnp.max(level, axis=0, keepdims=True))
    w = w / jnp.sum(w, axis=0, keepdims=True)
    w = jnp.concatenate([w, jnp.zeros((HD - parts, HD), F32)], axis=0).T
    for h in range(2):
        mixed = jnp.zeros((QN_DEV, HD), F32)
        for k in range(parts):
            column = w[h * QN_DEV:(h + 1) * QN_DEV, k:k + 1]
            mixed += column * in_ref[k, :QN_DEV, h * HD:(h + 1) * HD].astype(F32)
        out_ref[:, h * HD:(h + 1) * HD] = mixed.astype(BF)


def ctx_kernel(q_ref, kv_ref, info_ref, ctx_hbm, ctx_ref, local_ref, sems):
    alone = info_ref[0] == 0
    own = info_ref[1]
    stores = []
    for y in range(KVH):
        for g in range(N_LANE):
            to = (y * N_LANE + g) * BLK_DEV
            side = jnp.bitwise_xor(info_ref[2], g // 2)
            at = pl.multiple_of((g % 2 * 4 + side) * SHARE + y * BLK_DEV, BLK_DEV)
            local_ref[to:to + BLK_DEV, :] = kv_ref[pl.ds(at, BLK_DEV), :]
    anchor = jnp.concatenate(
        [kv_ref[(4 * c + 2) * SHARE:(4 * c + 4) * SHARE, :] for c in range(2)], axis=0
    )
    anchor_key, anchor_value = anchor[:, :HD], with_ones(anchor[:, HD:])
    step = CTX_ROWS
    col = lax.broadcasted_iota(jnp.int32, (1, ROWS), 1)
    spot = jnp.where(col < own, col, FAR)

    def score(i):
        rows = slice(i * step, (i + 1) * step)
        q = jnp.concatenate([q_ref[rows, :HD], q_ref[rows, HD:]], axis=0)
        a = lax.dot_general(q, anchor_key, NT, preferred_element_type=F32)
        b = lax.dot_general(q, local_ref[:(i + 1) * step, :HD], NT, preferred_element_type=F32)
        return a, b

    def finish(i, a, b):
        n = (i + 1) * step
        rows = slice(i * step, n)
        row = lax.broadcasted_iota(jnp.int32, (2 * step, n), 0) % step + i * step
        b = jnp.where(spot[:, :n] <= row, b, NEG)
        top_a = jnp.max(a, axis=1, keepdims=True)
        top = jnp.maximum(jnp.where(alone, NEG, top_a), jnp.max(b, axis=1, keepdims=True))
        a = jnp.exp2((a - jnp.where(alone, -NEG, top)) * SCALE2).astype(BF)
        b = jnp.exp2((b - top) * SCALE2).astype(BF)
        mixed = jnp.dot(a, anchor_value, preferred_element_type=F32)
        mixed += jnp.dot(b, with_ones(local_ref[:n, HD:]), preferred_element_type=F32)
        mean = (mixed[:, :HD] / mixed[:, HD:]).astype(BF)
        ctx_ref[rows, :HD] = mean[:step]
        ctx_ref[rows, HD:] = mean[step:]
        part = pl.ds(i * step, step)
        copy = pltpu.make_async_copy(ctx_ref.at[part], ctx_hbm.at[part], sems.at[i])
        copy.start()
        stores.append(copy)

    count = ROWS // step
    ahead = score(0)
    for i in range(count):
        a, b = ahead
        if i + 1 < count:
            ahead = score(i + 1)
        finish(i, a, b)
    for copy in stores:
        copy.wait()


def groups():
    z, x, y, g = range(N_Z), range(N_PAIR), range(KVH), range(N_LANE)
    at = lambda c, d, e, f: (c * N_PAIR + d) * KVH * N_LANE + e * N_LANE + f
    plane = [[at(c, d, e, f) for c in z for e in y] for d in x for f in g]
    line = [[at(c, d, e, f) for d in x for f in g] for c in z for e in y]
    four = [[e * N_LANE + f for f in g] for e in y]
    side = [[at(c, d, e, 2 * f + k) for d in x for f in range(2)] for c in z for e in y for k in range(2)]
    chip = [[2 * f, 2 * f + 1] for f in range(KVH * N_LANE // 2)]
    pairs = [[2 * c, 2 * c + 1] for c in z]
    return plane, line, four, side, chip, pairs


def solution(mesh):
    plane, line, four, side, chip, pairs = groups()
    both = ("hst", "dev")

    def per_device(ctx_query, ctx_key, ctx_value, query, block_lengths, query_positions):
        host = lax.axis_index("hst")
        z, pair = host // N_PAIR, host % N_PAIR
        smem = pl.BlockSpec(memory_space=pltpu.SMEM)
        vmem = pl.BlockSpec(memory_space=pltpu.VMEM)
        hbm = pl.BlockSpec(memory_space=pltpu.HBM)
        params = pltpu.CompilerParams(vmem_limit_bytes=VMEM_LIMIT)
        heavy = pl.CostEstimate(
            flops=800_000_000, bytes_accessed=1_200_000, transcendentals=1 << 20
        )
        dma = pltpu.SemaphoreType.DMA
        shape = lambda dims, dtype: jax.ShapeDtypeStruct(dims, dtype)

        send = pl.pallas_call(
            pack_kernel,
            out_shape=shape((N_Z * KVH, BLK_DEV, 2 * HD), BF),
            in_specs=[hbm, hbm],
            out_specs=hbm,
            scratch_shapes=[
                pltpu.VMEM(ctx_key.shape, BF),
                pltpu.VMEM(ctx_value.shape, BF),
                pltpu.VMEM((KVH, BLK_DEV, 2 * HD), BF),
                dma((2 + N_Z,)),
            ],
        )(ctx_key, ctx_value)
        share = lax.all_to_all(send, both, 0, 0, axis_index_groups=plane)
        share = share.reshape(N_Z * SHARE, 2 * HD)

        couple = lax.all_gather(query, "hst", axis=0, tiled=True, axis_index_groups=pairs)
        seen = lax.all_gather(couple, "dev", axis=0, tiled=True, axis_index_groups=four)
        place = jnp.stack([z, pair, lax.axis_index("dev") % N_LANE, jnp.zeros_like(z)])
        spans = N_PAIR * QN_DEV
        ask, spot, limits, info = pl.pallas_call(
            prep_kernel,
            out_shape=(
                shape((N_PAIR, 2 * N_LANE * QN_DEV, HD), BF),
                shape((8, N_Z * SHARE), F32),
                shape((spans, spans), F32),
                shape((3,), jnp.int32),
            ),
            in_specs=[vmem, vmem, smem, smem],
            out_specs=(vmem, vmem, vmem, smem),
            compiler_params=params,
        )(seen, query_positions.reshape(N_Z, spans), block_lengths, place)

        share, ask, spot, limits, info = lax.optimization_barrier(
            (share, ask, spot, limits, info)
        )
        local = lax.dynamic_slice_in_dim(share, z * SHARE, SHARE, 0)
        mine = jnp.concatenate([local, share[:SHARE]], axis=0)
        hosts, lanes = range(N_Z * N_PAIR), range(KVH * N_LANE)
        first = share[:SHARE]
        flip = lax.ppermute(mine, "dev", [(i, i ^ 2) for i in lanes])
        cross = lax.ppermute(first, "hst", [(i, i + 1) for i in hosts if i % 2 == 0])
        skew = lax.ppermute(
            first, both,
            [(i * len(lanes) + j, (i + 1) * len(lanes) + (j ^ 2)) for i in hosts if i % 2 == 0 for j in lanes],
        )

        dests = N_PAIR * N_LANE
        piece = (dests, QN_DEV + STAT, 2 * HD)
        partial = pl.pallas_call(
            far_kernel,
            out_shape=shape(piece, BF),
            in_specs=[vmem, vmem, vmem, vmem],
            out_specs=hbm,
            scratch_shapes=[pltpu.VMEM(piece, BF), dma((dests,))],
            compiler_params=params,
            cost_estimate=heavy,
        )(ask, share, spot, limits)
        partial, flip, cross, skew = lax.optimization_barrier((partial, flip, cross, skew))
        near_anchor = jnp.where(pair == 0, first, cross)
        far_anchor = jnp.where(pair == 0, flip[SHARE:], skew)
        near = lax.all_gather(
            jnp.concatenate([local, flip[:SHARE], near_anchor, far_anchor], axis=0),
            "dev", axis=0, tiled=True, axis_index_groups=chip,
        )
        arrived = lax.all_to_all(partial, both, 0, 0, axis_index_groups=line)

        ctx_out = pl.pallas_call(
            ctx_kernel,
            out_shape=shape(ctx_query.shape, BF),
            in_specs=[vmem, vmem, smem],
            out_specs=hbm,
            scratch_shapes=[
                pltpu.VMEM(ctx_query.shape, BF),
                pltpu.VMEM((ROWS, 2 * HD), BF),
                dma((ROWS // CTX_ROWS,)),
            ],
            compiler_params=params,
            cost_estimate=heavy,
        )(ctx_query, near, info)
        query_out = pl.pallas_call(
            merge_kernel,
            out_shape=shape(query.shape, BF),
            in_specs=[vmem],
            out_specs=vmem,
            compiler_params=params,
        )(arrived)
        return ctx_out, query_out

    return jax.shard_map(
        per_device,
        mesh=mesh,
        in_specs=(
            P("hst", "dev"),
            P(("hst", "dev"), None),
            P(("hst", "dev"), None),
            P("hst", "dev"),
            P(),
            P(),
        ),
        out_specs=(P("hst", "dev"), P("hst", "dev")),
        check_vma=False,
    )
```

```python
import math

import jax
import jax.numpy as jnp
from jax import lax
from jax.experimental import pallas as pl
from jax.experimental.pallas import tpu as pltpu
from jax.sharding import PartitionSpec as P

H = 64
KVH = 8
HD = 128
N_Z = 8
N_PAIR = 2
N_LANE = 4
BLK_DEV = 16
QN_DEV = 64
ROWS = 512
SHARE = KVH * BLK_DEV
STAT = 16

FAR_ROWS = 256
CTX_ROWS = 128
NEG = -1e30
FAR = 1 << 20
SCALE2 = HD ** (-0.5) * math.log2(math.e)
BF = jnp.bfloat16
F32 = jnp.float32
NT = (((1,), (1,)), ((), ()))
VMEM_LIMIT = 48 * 1024 * 1024


def pack_kernel(key_hbm, value_hbm, out_hbm, key_ref, value_ref, out_ref, sems):
    fetch = [
        pltpu.make_async_copy(key_hbm, key_ref, sems.at[0]),
        pltpu.make_async_copy(value_hbm, value_ref, sems.at[1]),
    ]
    for copy in fetch:
        copy.start()
    for copy in fetch:
        copy.wait()
    for head in range(KVH):
        cols = slice(head * HD, (head + 1) * HD)
        out_ref[head] = jnp.concatenate([key_ref[:, cols], value_ref[:, cols]], axis=1)
    store = [
        pltpu.make_async_copy(out_ref, out_hbm.at[pl.ds(z * KVH, KVH)], sems.at[2 + z])
        for z in range(N_Z)
    ]
    for copy in store:
        copy.start()
    for copy in store:
        copy.wait()


def with_ones(values):
    return jnp.concatenate([values, jnp.ones_like(values)], axis=1)


def prep_kernel(seen_ref, pos_ref, len_ref, place_ref, q_ref, spot_ref, lim_ref, info_ref):
    z = place_ref[0]
    pair = place_ref[1]
    lane = place_ref[2]
    info_ref[0] = z * N_PAIR + pair
    info_ref[1] = len_ref[z * N_PAIR + pair]
    info_ref[2] = lane // 2
    for g in range(N_LANE):
        for p in range(N_PAIR):
            at = (g * N_PAIR + p) * QN_DEV
            for h in range(2):
                rows = slice((2 * g + h) * QN_DEV, (2 * g + h + 1) * QN_DEV)
                q_ref[p, rows] = seen_ref[at:at + QN_DEV, h * HD:(h + 1) * HD]
    n = lax.broadcasted_iota(jnp.int32, spot_ref.shape, 1)
    host = (n // SHARE) * N_PAIR + pair
    inner = ((n % SHARE) // BLK_DEV * N_LANE + lane) * BLK_DEV + n % BLK_DEV
    length = jnp.zeros(spot_ref.shape, jnp.int32)
    for h in range(N_Z):
        length = jnp.where(n // SHARE == h, len_ref[h * N_PAIR + pair], length)
    spot_ref[...] = jnp.where(inner < length, host * ROWS + inner, FAR).astype(F32)
    lim_ref[...] = jnp.broadcast_to(pos_ref[pl.ds(z, 1), :].astype(F32), (HD, HD)).T


def far_kernel(q_ref, kv_ref, spot_ref, lim_ref, out_hbm, out_ref, sems):
    count = kv_ref.shape[0]
    spot = spot_ref[0:1, :]
    keys = kv_ref[:, :HD]
    values = with_ones(kv_ref[:, HD:])
    per = FAR_ROWS // QN_DEV
    blocks = [(p, r) for p in range(N_PAIR) for r in range(0, 2 * N_LANE * QN_DEV, FAR_ROWS)]
    stores = []

    def score(block):
        p, r = block
        return lax.dot_general(
            q_ref[p, r:r + FAR_ROWS], keys, NT, preferred_element_type=F32
        )

    def finish(block, s):
        p, r = block
        lim = lim_ref[p * QN_DEV:(p + 1) * QN_DEV, :]
        lim = jnp.concatenate([jnp.concatenate([lim] * per, axis=0)] * (count // HD), axis=1)
        s = jnp.where(spot < lim, s, NEG)
        top = jnp.max(s, axis=1, keepdims=True)
        w = jnp.exp2((s - top) * SCALE2).astype(BF)
        mixed = jnp.dot(w, values, preferred_element_type=F32)
        total = mixed[:, HD:]
        level = top * SCALE2 + jnp.log2(total)
        mean = (mixed[:, :HD] / total).astype(BF)
        first = p * N_LANE + r // (2 * QN_DEV)
        for j in range(per // 2):
            d = first + j
            base = j * 2 * QN_DEV
            out_ref[d, :QN_DEV, :HD] = mean[base:base + QN_DEV]
            out_ref[d, :QN_DEV, HD:] = mean[base + QN_DEV:base + 2 * QN_DEV]
            flat = level[base:base + 2 * QN_DEV].T[:STAT]
            high = flat.astype(BF).astype(F32)
            rest = flat - high
            mid = rest.astype(BF).astype(F32)
            row = lax.broadcasted_iota(jnp.int32, (STAT, HD), 0)
            stat = jnp.where(row == 0, high, jnp.where(row == 1, mid, rest - mid))
            out_ref[d, QN_DEV:, :HD] = stat.astype(BF)
            out_ref[d, QN_DEV:, HD:] = jnp.zeros((STAT, HD), BF)
        part = pl.ds(first, per // 2)
        copy = pltpu.make_async_copy(out_ref.at[part], out_hbm.at[part], sems.at[len(stores)])
        copy.start()
        stores.append(copy)

    ahead = score(blocks[0])
    for k, block in enumerate(blocks):
        s = ahead
        if k + 1 < len(blocks):
            ahead = score(blocks[k + 1])
        finish(block, s)
    for copy in stores:
        copy.wait()


def merge_kernel(in_ref, out_ref):
    parts = in_ref.shape[0]
    levels = []
    for k in range(parts):
        stat = in_ref[k, QN_DEV:, :HD].astype(F32)
        levels.append(stat[0:1] + stat[1:2] + stat[2:3])
    level = jnp.concatenate(levels, axis=0)
    w = jnp.exp2(level - jnp.max(level, axis=0, keepdims=True))
    w = w / jnp.sum(w, axis=0, keepdims=True)
    w = jnp.concatenate([w, jnp.zeros((HD - parts, HD), F32)], axis=0).T
    for h in range(2):
        mixed = jnp.zeros((QN_DEV, HD), F32)
        for k in range(parts):
            column = w[h * QN_DEV:(h + 1) * QN_DEV, k:k + 1]
            mixed += column * in_ref[k, :QN_DEV, h * HD:(h + 1) * HD].astype(F32)
        out_ref[:, h * HD:(h + 1) * HD] = mixed.astype(BF)


def ctx_kernel(q_ref, kv_ref, info_ref, ctx_hbm, ctx_ref, local_ref, sems):
    alone = info_ref[0] == 0
    own = info_ref[1]
    stores = []
    for y in range(KVH):
        for g in range(N_LANE):
            to = (y * N_LANE + g) * BLK_DEV
            side = jnp.bitwise_xor(info_ref[2], g // 2)
            at = pl.multiple_of((g % 2 * 4 + side) * SHARE + y * BLK_DEV, BLK_DEV)
            local_ref[to:to + BLK_DEV, :] = kv_ref[pl.ds(at, BLK_DEV), :]
    anchor = jnp.concatenate(
        [kv_ref[(4 * c + 2) * SHARE:(4 * c + 4) * SHARE, :] for c in range(2)], axis=0
    )
    anchor_key, anchor_value = anchor[:, :HD], with_ones(anchor[:, HD:])
    step = CTX_ROWS
    col = lax.broadcasted_iota(jnp.int32, (1, ROWS), 1)
    spot = jnp.where(col < own, col, FAR)

    def score(i):
        rows = slice(i * step, (i + 1) * step)
        q = jnp.concatenate([q_ref[rows, :HD], q_ref[rows, HD:]], axis=0)
        a = lax.dot_general(q, anchor_key, NT, preferred_element_type=F32)
        b = lax.dot_general(q, local_ref[:(i + 1) * step, :HD], NT, preferred_element_type=F32)
        return a, b

    def finish(i, a, b):
        n = (i + 1) * step
        rows = slice(i * step, n)
        row = lax.broadcasted_iota(jnp.int32, (2 * step, n), 0) % step + i * step
        b = jnp.where(spot[:, :n] <= row, b, NEG)
        top_a = jnp.max(a, axis=1, keepdims=True)
        top = jnp.maximum(jnp.where(alone, NEG, top_a), jnp.max(b, axis=1, keepdims=True))
        a = jnp.exp2((a - jnp.where(alone, -NEG, top)) * SCALE2).astype(BF)
        b = jnp.exp2((b - top) * SCALE2).astype(BF)
        mixed = jnp.dot(a, anchor_value, preferred_element_type=F32)
        mixed += jnp.dot(b, with_ones(local_ref[:n, HD:]), preferred_element_type=F32)
        mean = (mixed[:, :HD] / mixed[:, HD:]).astype(BF)
        ctx_ref[rows, :HD] = mean[:step]
        ctx_ref[rows, HD:] = mean[step:]
        part = pl.ds(i * step, step)
        copy = pltpu.make_async_copy(ctx_ref.at[part], ctx_hbm.at[part], sems.at[i])
        copy.start()
        stores.append(copy)

    count = ROWS // step
    ahead = score(0)
    for i in range(count):
        a, b = ahead
        if i + 1 < count:
            ahead = score(i + 1)
        finish(i, a, b)
    for copy in stores:
        copy.wait()


def groups():
    z, x, y, g = range(N_Z), range(N_PAIR), range(KVH), range(N_LANE)
    at = lambda c, d, e, f: (c * N_PAIR + d) * KVH * N_LANE + e * N_LANE + f
    plane = [[at(c, d, e, f) for c in z for e in y] for d in x for f in g]
    line = [[at(c, d, e, f) for d in x for f in g] for c in z for e in y]
    four = [[e * N_LANE + f for f in g] for e in y]
    side = [[at(c, d, e, 2 * f + k) for d in x for f in range(2)] for c in z for e in y for k in range(2)]
    chip = [[2 * f, 2 * f + 1] for f in range(KVH * N_LANE // 2)]
    pairs = [[2 * c, 2 * c + 1] for c in z]
    return plane, line, four, side, chip, pairs


def solution(mesh):
    plane, line, four, side, chip, pairs = groups()
    both = ("hst", "dev")

    def per_device(ctx_query, ctx_key, ctx_value, query, block_lengths, query_positions):
        host = lax.axis_index("hst")
        z, pair = host // N_PAIR, host % N_PAIR
        smem = pl.BlockSpec(memory_space=pltpu.SMEM)
        vmem = pl.BlockSpec(memory_space=pltpu.VMEM)
        hbm = pl.BlockSpec(memory_space=pltpu.HBM)
        params = pltpu.CompilerParams(vmem_limit_bytes=VMEM_LIMIT)
        heavy = pl.CostEstimate(
            flops=800_000_000, bytes_accessed=1_200_000, transcendentals=1 << 20
        )
        dma = pltpu.SemaphoreType.DMA
        shape = lambda dims, dtype: jax.ShapeDtypeStruct(dims, dtype)

        send = pl.pallas_call(
            pack_kernel,
            out_shape=shape((N_Z * KVH, BLK_DEV, 2 * HD), BF),
            in_specs=[hbm, hbm],
            out_specs=hbm,
            scratch_shapes=[
                pltpu.VMEM(ctx_key.shape, BF),
                pltpu.VMEM(ctx_value.shape, BF),
                pltpu.VMEM((KVH, BLK_DEV, 2 * HD), BF),
                dma((2 + N_Z,)),
            ],
        )(ctx_key, ctx_value)
        share = lax.all_to_all(send, both, 0, 0, axis_index_groups=plane)
        share = share.reshape(N_Z * SHARE, 2 * HD)

        couple = lax.all_gather(query, "hst", axis=0, tiled=True, axis_index_groups=pairs)
        seen = lax.all_gather(couple, "dev", axis=0, tiled=True, axis_index_groups=four)
        place = jnp.stack([z, pair, lax.axis_index("dev") % N_LANE, jnp.zeros_like(z)])
        spans = N_PAIR * QN_DEV
        ask, spot, limits, info = pl.pallas_call(
            prep_kernel,
            out_shape=(
                shape((N_PAIR, 2 * N_LANE * QN_DEV, HD), BF),
                shape((8, N_Z * SHARE), F32),
                shape((spans, spans), F32),
                shape((3,), jnp.int32),
            ),
            in_specs=[vmem, vmem, smem, smem],
            out_specs=(vmem, vmem, vmem, smem),
            compiler_params=params,
        )(seen, query_positions.reshape(N_Z, spans), block_lengths, place)

        share, ask, spot, limits, info = lax.optimization_barrier(
            (share, ask, spot, limits, info)
        )
        local = lax.dynamic_slice_in_dim(share, z * SHARE, SHARE, 0)
        mine = jnp.concatenate([local, share[:SHARE]], axis=0)
        hosts, lanes = range(N_Z * N_PAIR), range(KVH * N_LANE)
        first = share[:SHARE]
        flip = lax.ppermute(mine, "dev", [(i, i ^ 2) for i in lanes])

        dests = N_PAIR * N_LANE
        piece = (dests, QN_DEV + STAT, 2 * HD)
        partial = pl.pallas_call(
            far_kernel,
            out_shape=shape(piece, BF),
            in_specs=[vmem, vmem, vmem, vmem],
            out_specs=hbm,
            scratch_shapes=[pltpu.VMEM(piece, BF), dma((dests,))],
            compiler_params=params,
            cost_estimate=heavy,
        )(ask, share, spot, limits)
        partial, anchor = lax.optimization_barrier((partial, first))
        cross = lax.ppermute(anchor, "hst", [(i, i + 1) for i in hosts if i % 2 == 0])
        skew = lax.ppermute(
            anchor, both,
            [(i * len(lanes) + j, (i + 1) * len(lanes) + (j ^ 2)) for i in hosts if i % 2 == 0 for j in lanes],
        )
        flip, cross, skew = lax.optimization_barrier((flip, cross, skew))
        near_anchor = jnp.where(pair == 0, first, cross)
        far_anchor = jnp.where(pair == 0, flip[SHARE:], skew)
        near = lax.all_gather(
            jnp.concatenate([local, flip[:SHARE], near_anchor, far_anchor], axis=0),
            "dev", axis=0, tiled=True, axis_index_groups=chip,
        )
        arrived = lax.all_to_all(partial, both, 0, 0, axis_index_groups=line)

        ctx_out = pl.pallas_call(
            ctx_kernel,
            out_shape=shape(ctx_query.shape, BF),
            in_specs=[vmem, vmem, smem],
            out_specs=hbm,
            scratch_shapes=[
                pltpu.VMEM(ctx_query.shape, BF),
                pltpu.VMEM((ROWS, 2 * HD), BF),
                dma((ROWS // CTX_ROWS,)),
            ],
            compiler_params=params,
            cost_estimate=heavy,
        )(ctx_query, near, info)
        query_out = pl.pallas_call(
            merge_kernel,
            out_shape=shape(query.shape, BF),
            in_specs=[vmem],
            out_specs=vmem,
            compiler_params=params,
        )(arrived)
        return ctx_out, query_out

    return jax.shard_map(
        per_device,
        mesh=mesh,
        in_specs=(
            P("hst", "dev"),
            P(("hst", "dev"), None),
            P(("hst", "dev"), None),
            P("hst", "dev"),
            P(),
            P(),
        ),
        out_specs=(P("hst", "dev"), P("hst", "dev")),
        check_vma=False,
    )
```

```python
import math

import jax
import jax.numpy as jnp
from jax import lax
from jax.experimental import pallas as pl
from jax.experimental.pallas import tpu as pltpu
from jax.sharding import PartitionSpec as P

H = 64
KVH = 8
HD = 128
N_Z = 8
N_PAIR = 2
N_LANE = 4
BLK_DEV = 16
QN_DEV = 64
ROWS = 512
SHARE = KVH * BLK_DEV
STAT = 16

FAR_BLOCKS = ((0, 0, 128), (0, 128, 256), (0, 384, 128), (1, 0, 256), (1, 256, 128), (1, 384, 128))
CTX_ROWS = 128
NEG = -1e30
FAR = 1 << 20
SCALE2 = HD ** (-0.5) * math.log2(math.e)
BF = jnp.bfloat16
F32 = jnp.float32
NT = (((1,), (1,)), ((), ()))
VMEM_LIMIT = 48 * 1024 * 1024


def pack_kernel(key_hbm, value_hbm, out_hbm, key_ref, value_ref, out_ref, sems):
    fetch = [
        pltpu.make_async_copy(key_hbm, key_ref, sems.at[0]),
        pltpu.make_async_copy(value_hbm, value_ref, sems.at[1]),
    ]
    for copy in fetch:
        copy.start()
    for copy in fetch:
        copy.wait()
    for head in range(KVH):
        cols = slice(head * HD, (head + 1) * HD)
        out_ref[head] = jnp.concatenate([key_ref[:, cols], value_ref[:, cols]], axis=1)
    store = [
        pltpu.make_async_copy(out_ref, out_hbm.at[pl.ds(z * KVH, KVH)], sems.at[2 + z])
        for z in range(N_Z)
    ]
    for copy in store:
        copy.start()
    for copy in store:
        copy.wait()


def with_ones(values):
    return jnp.concatenate([values, jnp.ones_like(values)], axis=1)


def prep_kernel(seen_ref, pos_ref, len_ref, place_ref, q_ref, spot_ref, lim_ref, own_ref, gate_ref):
    z = place_ref[0]
    pair = place_ref[1]
    lane = place_ref[2]
    here = z * N_PAIR + pair
    col = lax.broadcasted_iota(jnp.int32, own_ref.shape, 1)
    own_ref[...] = jnp.where(col < len_ref[here], col, FAR).astype(F32)
    gate_ref[...] = jnp.full(gate_ref.shape, jnp.where(here == 0, -NEG, 0.0), F32)
    for g in range(N_LANE):
        for p in range(N_PAIR):
            at = (g * N_PAIR + p) * QN_DEV
            for h in range(2):
                rows = slice((2 * g + h) * QN_DEV, (2 * g + h + 1) * QN_DEV)
                q_ref[p, rows] = seen_ref[at:at + QN_DEV, h * HD:(h + 1) * HD]
    n = lax.broadcasted_iota(jnp.int32, spot_ref.shape, 1)
    host = (n // SHARE) * N_PAIR + pair
    inner = ((n % SHARE) // BLK_DEV * N_LANE + lane) * BLK_DEV + n % BLK_DEV
    length = jnp.zeros(spot_ref.shape, jnp.int32)
    for h in range(N_Z):
        length = jnp.where(n // SHARE == h, len_ref[h * N_PAIR + pair], length)
    spot_ref[...] = jnp.where(inner < length, host * ROWS + inner, FAR).astype(F32)
    lim_ref[...] = jnp.broadcast_to(pos_ref[pl.ds(z, 1), :].astype(F32), (HD, HD)).T


def far_kernel(q_ref, kv_ref, spot_ref, lim_ref, out_hbm, out_ref, sems):
    count = kv_ref.shape[0]
    spot = spot_ref[0:1, :]
    keys = kv_ref[:, :HD]
    values = with_ones(kv_ref[:, HD:])
    blocks = FAR_BLOCKS
    stores = []

    def score(block):
        p, r, size = block
        return lax.dot_general(
            q_ref[p, r:r + size], keys, NT, preferred_element_type=F32
        )

    def finish(block, s):
        p, r, size = block
        per = size // QN_DEV
        lim = lim_ref[p * QN_DEV:(p + 1) * QN_DEV, :]
        lim = jnp.concatenate([jnp.concatenate([lim] * per, axis=0)] * (count // HD), axis=1)
        s = jnp.where(spot < lim, s, NEG)
        top = jnp.max(s, axis=1, keepdims=True)
        w = jnp.exp2((s - top) * SCALE2).astype(BF)
        mixed = jnp.dot(w, values, preferred_element_type=F32)
        total = mixed[:, HD:]
        level = top * SCALE2 + jnp.log2(total)
        mean = (mixed[:, :HD] / total).astype(BF)
        first = p * N_LANE + r // (2 * QN_DEV)
        for j in range(per // 2):
            d = first + j
            base = j * 2 * QN_DEV
            out_ref[d, :QN_DEV, :HD] = mean[base:base + QN_DEV]
            out_ref[d, :QN_DEV, HD:] = mean[base + QN_DEV:base + 2 * QN_DEV]
            flat = level[base:base + 2 * QN_DEV].T[:STAT]
            high = flat.astype(BF).astype(F32)
            rest = flat - high
            mid = rest.astype(BF).astype(F32)
            row = lax.broadcasted_iota(jnp.int32, (STAT, HD), 0)
            stat = jnp.where(row == 0, high, jnp.where(row == 1, mid, rest - mid))
            out_ref[d, QN_DEV:, :HD] = stat.astype(BF)
            out_ref[d, QN_DEV:, HD:] = jnp.zeros((STAT, HD), BF)
        part = pl.ds(first, per // 2)
        copy = pltpu.make_async_copy(out_ref.at[part], out_hbm.at[part], sems.at[len(stores)])
        copy.start()
        stores.append(copy)

    ahead = score(blocks[0])
    for k, block in enumerate(blocks):
        s = ahead
        if k + 1 < len(blocks):
            ahead = score(blocks[k + 1])
        finish(block, s)
    for copy in stores:
        copy.wait()


def merge_kernel(in_ref, out_ref):
    parts = in_ref.shape[0]
    levels = []
    for k in range(parts):
        stat = in_ref[k, QN_DEV:, :HD].astype(F32)
        levels.append(stat[0:1] + stat[1:2] + stat[2:3])
    level = jnp.concatenate(levels, axis=0)
    w = jnp.exp2(level - jnp.max(level, axis=0, keepdims=True))
    w = w / jnp.sum(w, axis=0, keepdims=True)
    w = jnp.concatenate([w, jnp.zeros((HD - parts, HD), F32)], axis=0).T
    for h in range(2):
        mixed = jnp.zeros((QN_DEV, HD), F32)
        for k in range(parts):
            column = w[h * QN_DEV:(h + 1) * QN_DEV, k:k + 1]
            mixed += column * in_ref[k, :QN_DEV, h * HD:(h + 1) * HD].astype(F32)
        out_ref[:, h * HD:(h + 1) * HD] = mixed.astype(BF)


def ctx_kernel(q_ref, kv_ref, own_ref, gate_ref, ctx_hbm, ctx_ref, local_ref, sems):
    gate = gate_ref[0:1, 0:1]
    stores = []
    for y in range(KVH):
        for g in range(N_LANE):
            to = (y * N_LANE + g) * BLK_DEV
            at = (g % 2 * 4 + g // 2) * SHARE + y * BLK_DEV
            local_ref[to:to + BLK_DEV, :] = kv_ref[at:at + BLK_DEV, :]
    anchor = jnp.concatenate(
        [kv_ref[(4 * c + 2) * SHARE:(4 * c + 4) * SHARE, :] for c in range(2)], axis=0
    )
    anchor_key, anchor_value = anchor[:, :HD], with_ones(anchor[:, HD:])
    step = CTX_ROWS
    spot = own_ref[0:1, :]

    def score(i):
        rows = slice(i * step, (i + 1) * step)
        q = jnp.concatenate([q_ref[rows, :HD], q_ref[rows, HD:]], axis=0)
        a = lax.dot_general(q, anchor_key, NT, preferred_element_type=F32)
        b = lax.dot_general(q, local_ref[:(i + 1) * step, :HD], NT, preferred_element_type=F32)
        return a, b

    def finish(i, a, b):
        n = (i + 1) * step
        rows = slice(i * step, n)
        row = (lax.broadcasted_iota(jnp.int32, (2 * step, n), 0) % step + i * step).astype(F32)
        b = jnp.where(spot[:, :n] <= row, b, NEG)
        top_a = jnp.max(a, axis=1, keepdims=True)
        top = jnp.maximum(top_a - gate, jnp.max(b, axis=1, keepdims=True))
        a = jnp.exp2((a - (top + gate)) * SCALE2).astype(BF)
        b = jnp.exp2((b - top) * SCALE2).astype(BF)
        mixed = jnp.dot(a, anchor_value, preferred_element_type=F32)
        mixed += jnp.dot(b, with_ones(local_ref[:n, HD:]), preferred_element_type=F32)
        mean = (mixed[:, :HD] / mixed[:, HD:]).astype(BF)
        ctx_ref[rows, :HD] = mean[:step]
        ctx_ref[rows, HD:] = mean[step:]
        part = pl.ds(i * step, step)
        copy = pltpu.make_async_copy(ctx_ref.at[part], ctx_hbm.at[part], sems.at[i])
        copy.start()
        stores.append(copy)

    count = ROWS // step
    ahead = score(count - 1)
    for i in reversed(range(count)):
        a, b = ahead
        if i > 0:
            ahead = score(i - 1)
        finish(i, a, b)
    for copy in stores:
        copy.wait()


def groups():
    z, x, y, g = range(N_Z), range(N_PAIR), range(KVH), range(N_LANE)
    at = lambda c, d, e, f: (c * N_PAIR + d) * KVH * N_LANE + e * N_LANE + f
    plane = [[at(c, d, e, f) for c in z for e in y] for d in x for f in g]
    line = [[at(c, d, e, f) for d in x for f in g] for c in z for e in y]
    four = [[e * N_LANE + f for f in g] for e in y]
    side = [[at(c, d, e, 2 * f + k) for d in x for f in range(2)] for c in z for e in y for k in range(2)]
    chip = [[2 * f, 2 * f + 1] for f in range(KVH * N_LANE // 2)]
    pairs = [[2 * c, 2 * c + 1] for c in z]
    return plane, line, four, side, chip, pairs


def solution(mesh):
    plane, line, four, side, chip, pairs = groups()
    both = ("hst", "dev")

    def per_device(ctx_query, ctx_key, ctx_value, query, block_lengths, query_positions):
        host = lax.axis_index("hst")
        z, pair = host // N_PAIR, host % N_PAIR
        smem = pl.BlockSpec(memory_space=pltpu.SMEM)
        vmem = pl.BlockSpec(memory_space=pltpu.VMEM)
        hbm = pl.BlockSpec(memory_space=pltpu.HBM)
        params = pltpu.CompilerParams(vmem_limit_bytes=VMEM_LIMIT)
        heavy = pl.CostEstimate(
            flops=800_000_000, bytes_accessed=1_200_000, transcendentals=1 << 20
        )
        dma = pltpu.SemaphoreType.DMA
        shape = lambda dims, dtype: jax.ShapeDtypeStruct(dims, dtype)

        send = pl.pallas_call(
            pack_kernel,
            out_shape=shape((N_Z * KVH, BLK_DEV, 2 * HD), BF),
            in_specs=[hbm, hbm],
            out_specs=hbm,
            scratch_shapes=[
                pltpu.VMEM(ctx_key.shape, BF),
                pltpu.VMEM(ctx_value.shape, BF),
                pltpu.VMEM((KVH, BLK_DEV, 2 * HD), BF),
                dma((2 + N_Z,)),
            ],
        )(ctx_key, ctx_value)
        share = lax.all_to_all(send, both, 0, 0, axis_index_groups=plane)
        share = share.reshape(N_Z * SHARE, 2 * HD)

        couple = lax.all_gather(query, "hst", axis=0, tiled=True, axis_index_groups=pairs)
        seen = lax.all_gather(couple, "dev", axis=0, tiled=True, axis_index_groups=four)
        place = jnp.stack([z, pair, lax.axis_index("dev") % N_LANE, jnp.zeros_like(z)])
        spans = N_PAIR * QN_DEV
        ask, spot, limits, own_spot, gate = pl.pallas_call(
            prep_kernel,
            out_shape=(
                shape((N_PAIR, 2 * N_LANE * QN_DEV, HD), BF),
                shape((8, N_Z * SHARE), F32),
                shape((spans, spans), F32),
                shape((8, ROWS), F32),
                shape((8, HD), F32),
            ),
            in_specs=[vmem, vmem, smem, smem],
            out_specs=(vmem,) * 5,
            compiler_params=params,
        )(seen, query_positions.reshape(N_Z, spans), block_lengths, place)

        share, ask, spot, limits, own_spot, gate = lax.optimization_barrier(
            (share, ask, spot, limits, own_spot, gate)
        )
        local = lax.dynamic_slice_in_dim(share, z * SHARE, SHARE, 0)
        mine = jnp.concatenate([local, share[:SHARE]], axis=0)
        hosts, lanes = range(N_Z * N_PAIR), range(KVH * N_LANE)
        first = share[:SHARE]
        flip = lax.ppermute(mine, "dev", [(i, i ^ 2) for i in lanes])

        dests = N_PAIR * N_LANE
        piece = (dests, QN_DEV + STAT, 2 * HD)
        partial = pl.pallas_call(
            far_kernel,
            out_shape=shape(piece, BF),
            in_specs=[vmem, vmem, vmem, vmem],
            out_specs=hbm,
            scratch_shapes=[pltpu.VMEM(piece, BF), dma((dests,))],
            compiler_params=params,
            cost_estimate=heavy,
        )(ask, share, spot, limits)
        partial, anchor = lax.optimization_barrier((partial, first))
        cross = lax.ppermute(anchor, "hst", [(i, i + 1) for i in hosts if i % 2 == 0])
        skew = lax.ppermute(
            anchor, both,
            [(i * len(lanes) + j, (i + 1) * len(lanes) + (j ^ 2)) for i in hosts if i % 2 == 0 for j in lanes],
        )
        flip, cross, skew = lax.optimization_barrier((flip, cross, skew))
        near_anchor = jnp.where(pair == 0, first, cross)
        far_anchor = jnp.where(pair == 0, flip[SHARE:], skew)
        even = lax.axis_index("dev") % N_LANE < 2
        other = flip[:SHARE]
        near = lax.all_gather(
            jnp.concatenate(
                [
                    jnp.where(even, local, other),
                    jnp.where(even, other, local),
                    near_anchor,
                    far_anchor,
                ],
                axis=0,
            ),
            "dev", axis=0, tiled=True, axis_index_groups=chip,
        )
        arrived = lax.all_to_all(partial, both, 0, 0, axis_index_groups=line)

        ctx_out = pl.pallas_call(
            ctx_kernel,
            out_shape=shape(ctx_query.shape, BF),
            in_specs=[vmem] * 4,
            out_specs=hbm,
            scratch_shapes=[
                pltpu.VMEM(ctx_query.shape, BF),
                pltpu.VMEM((ROWS, 2 * HD), BF),
                dma((ROWS // CTX_ROWS,)),
            ],
            compiler_params=params,
            cost_estimate=heavy,
        )(ctx_query, near, own_spot, gate)
        query_out = pl.pallas_call(
            merge_kernel,
            out_shape=shape(query.shape, BF),
            in_specs=[vmem],
            out_specs=vmem,
            compiler_params=params,
        )(arrived)
        return ctx_out, query_out

    return jax.shard_map(
        per_device,
        mesh=mesh,
        in_specs=(
            P("hst", "dev"),
            P(("hst", "dev"), None),
            P(("hst", "dev"), None),
            P("hst", "dev"),
            P(),
            P(),
        ),
        out_specs=(P("hst", "dev"), P("hst", "dev")),
        check_vma=False,
    )
```

```python
import math

import jax
import jax.numpy as jnp
from jax import lax
from jax.experimental import pallas as pl
from jax.experimental.pallas import tpu as pltpu
from jax.sharding import PartitionSpec as P

H = 64
KVH = 8
HD = 128
N_Z = 8
N_PAIR = 2
N_LANE = 4
BLK_DEV = 16
QN_DEV = 64
ROWS = 512
SHARE = KVH * BLK_DEV
STAT = 8

FAR_BLOCKS = ((0, 0, 128), (0, 128, 256), (0, 384, 128), (1, 0, 256), (1, 256, 128), (1, 384, 128))
CTX_ROWS = 128
NEG = -1e30
FAR = 1 << 20
SCALE2 = HD ** (-0.5) * math.log2(math.e)
BF = jnp.bfloat16
F32 = jnp.float32
NT = (((1,), (1,)), ((), ()))
VMEM_LIMIT = 48 * 1024 * 1024


def pack_kernel(key_hbm, value_hbm, out_hbm, key_ref, value_ref, out_ref, sems):
    fetch = [
        pltpu.make_async_copy(key_hbm, key_ref, sems.at[0]),
        pltpu.make_async_copy(value_hbm, value_ref, sems.at[1]),
    ]
    for copy in fetch:
        copy.start()
    for copy in fetch:
        copy.wait()
    for head in range(KVH):
        cols = slice(head * HD, (head + 1) * HD)
        out_ref[head] = jnp.concatenate([key_ref[:, cols], value_ref[:, cols]], axis=1)
    store = [
        pltpu.make_async_copy(out_ref, out_hbm.at[pl.ds(z * KVH, KVH)], sems.at[2 + z])
        for z in range(N_Z)
    ]
    for copy in store:
        copy.start()
    for copy in store:
        copy.wait()


def with_ones(values):
    return jnp.concatenate([values, jnp.ones_like(values)], axis=1)


def prep_kernel(seen_ref, pos_ref, len_ref, place_ref, q_ref, spot_ref, lim_ref, own_ref, gate_ref):
    z = place_ref[0]
    pair = place_ref[1]
    lane = place_ref[2]
    here = z * N_PAIR + pair
    col = lax.broadcasted_iota(jnp.int32, own_ref.shape, 1)
    own_ref[...] = jnp.where(col < len_ref[here], col, FAR).astype(F32)
    gate_ref[...] = jnp.full(gate_ref.shape, jnp.where(here == 0, -NEG, 0.0), F32)
    for g in range(N_LANE):
        for p in range(N_PAIR):
            at = (g * N_PAIR + p) * QN_DEV
            for h in range(2):
                rows = slice((2 * g + h) * QN_DEV, (2 * g + h + 1) * QN_DEV)
                q_ref[p, rows] = seen_ref[at:at + QN_DEV, h * HD:(h + 1) * HD]
    n = lax.broadcasted_iota(jnp.int32, spot_ref.shape, 1)
    host = (n // SHARE) * N_PAIR + pair
    inner = ((n % SHARE) // BLK_DEV * N_LANE + lane) * BLK_DEV + n % BLK_DEV
    length = jnp.zeros(spot_ref.shape, jnp.int32)
    for h in range(N_Z):
        length = jnp.where(n // SHARE == h, len_ref[h * N_PAIR + pair], length)
    spot_ref[...] = jnp.where(inner < length, host * ROWS + inner, FAR).astype(F32)
    lim_ref[...] = jnp.broadcast_to(pos_ref[pl.ds(z, 1), :].astype(F32), (HD, HD)).T


def far_kernel(q_ref, kv_ref, spot_ref, lim_ref, out_hbm, out_ref, sems):
    count = kv_ref.shape[0]
    spot = spot_ref[0:1, :]
    keys = kv_ref[:, :HD]
    values = with_ones(kv_ref[:, HD:])
    blocks = FAR_BLOCKS
    stores = []

    def score(block):
        p, r, size = block
        return lax.dot_general(
            q_ref[p, r:r + size], keys, NT, preferred_element_type=F32
        )

    def finish(block, s):
        p, r, size = block
        per = size // QN_DEV
        lim = lim_ref[p * QN_DEV:(p + 1) * QN_DEV, :]
        lim = jnp.concatenate([jnp.concatenate([lim] * per, axis=0)] * (count // HD), axis=1)
        s = jnp.where(spot < lim, s, NEG)
        top = jnp.max(s, axis=1, keepdims=True)
        w = jnp.exp2((s - top) * SCALE2).astype(BF)
        mixed = jnp.dot(w, values, preferred_element_type=F32)
        total = mixed[:, HD:]
        level = top * SCALE2 + jnp.log2(total)
        mean = (mixed[:, :HD] / total).astype(BF)
        first = p * N_LANE + r // (2 * QN_DEV)
        for j in range(per // 2):
            d = first + j
            base = j * 2 * QN_DEV
            out_ref[d, :QN_DEV, :HD] = mean[base:base + QN_DEV]
            out_ref[d, :QN_DEV, HD:] = mean[base + QN_DEV:base + 2 * QN_DEV]
            flat = level[base:base + 2 * QN_DEV].T[:STAT]
            high = flat.astype(BF).astype(F32)
            rest = flat - high
            mid = rest.astype(BF).astype(F32)
            row = lax.broadcasted_iota(jnp.int32, (STAT, HD), 0)
            stat = jnp.where(row == 0, high, jnp.where(row == 1, mid, rest - mid))
            out_ref[d, QN_DEV:, :HD] = stat.astype(BF)
            out_ref[d, QN_DEV:, HD:] = jnp.zeros((STAT, HD), BF)
        part = pl.ds(first, per // 2)
        copy = pltpu.make_async_copy(out_ref.at[part], out_hbm.at[part], sems.at[len(stores)])
        copy.start()
        stores.append(copy)

    ahead = score(blocks[0])
    for k, block in enumerate(blocks):
        s = ahead
        if k + 1 < len(blocks):
            ahead = score(blocks[k + 1])
        finish(block, s)
    for copy in stores:
        copy.wait()


def merge_kernel(in_ref, out_ref):
    parts = in_ref.shape[0]
    levels = []
    for k in range(parts):
        stat = in_ref[k, QN_DEV:, :HD].astype(F32)
        levels.append(stat[0:1] + stat[1:2] + stat[2:3])
    level = jnp.concatenate(levels, axis=0)
    w = jnp.exp2(level - jnp.max(level, axis=0, keepdims=True))
    w = w / jnp.sum(w, axis=0, keepdims=True)
    w = jnp.concatenate([w, jnp.zeros((HD - parts, HD), F32)], axis=0).T
    for h in range(2):
        mixed = jnp.zeros((QN_DEV, HD), F32)
        for k in range(parts):
            column = w[h * QN_DEV:(h + 1) * QN_DEV, k:k + 1]
            mixed += column * in_ref[k, :QN_DEV, h * HD:(h + 1) * HD].astype(F32)
        out_ref[:, h * HD:(h + 1) * HD] = mixed.astype(BF)


def ctx_kernel(q_ref, kv_ref, own_ref, gate_ref, ctx_hbm, ctx_ref, local_ref, sems):
    gate = gate_ref[0:1, 0:1]
    stores = []
    for y in range(KVH):
        for g in range(N_LANE):
            to = (y * N_LANE + g) * BLK_DEV
            at = (g % 2 * 4 + g // 2) * SHARE + y * BLK_DEV
            local_ref[to:to + BLK_DEV, :] = kv_ref[at:at + BLK_DEV, :]
    anchor = jnp.concatenate(
        [kv_ref[(4 * c + 2) * SHARE:(4 * c + 4) * SHARE, :] for c in range(2)], axis=0
    )
    anchor_key, anchor_value = anchor[:, :HD], with_ones(anchor[:, HD:])
    step = CTX_ROWS
    spot = own_ref[0:1, :]

    def score(i):
        rows = slice(i * step, (i + 1) * step)
        q = jnp.concatenate([q_ref[rows, :HD], q_ref[rows, HD:]], axis=0)
        a = lax.dot_general(q, anchor_key, NT, preferred_element_type=F32)
        b = lax.dot_general(q, local_ref[:(i + 1) * step, :HD], NT, preferred_element_type=F32)
        return a, b

    def finish(i, a, b):
        n = (i + 1) * step
        rows = slice(i * step, n)
        row = (lax.broadcasted_iota(jnp.int32, (2 * step, n), 0) % step + i * step).astype(F32)
        b = jnp.where(spot[:, :n] <= row, b, NEG)
        top_a = jnp.max(a, axis=1, keepdims=True)
        top = jnp.maximum(top_a - gate, jnp.max(b, axis=1, keepdims=True))
        a = jnp.exp2((a - (top + gate)) * SCALE2).astype(BF)
        b = jnp.exp2((b - top) * SCALE2).astype(BF)
        mixed = jnp.dot(a, anchor_value, preferred_element_type=F32)
        mixed += jnp.dot(b, with_ones(local_ref[:n, HD:]), preferred_element_type=F32)
        mean = (mixed[:, :HD] / mixed[:, HD:]).astype(BF)
        ctx_ref[rows, :HD] = mean[:step]
        ctx_ref[rows, HD:] = mean[step:]
        part = pl.ds(i * step, step)
        copy = pltpu.make_async_copy(ctx_ref.at[part], ctx_hbm.at[part], sems.at[i])
        copy.start()
        stores.append(copy)

    count = ROWS // step
    ahead = score(count - 1)
    for i in reversed(range(count)):
        a, b = ahead
        if i > 0:
            ahead = score(i - 1)
        finish(i, a, b)
    for copy in stores:
        copy.wait()


def groups():
    z, x, y, g = range(N_Z), range(N_PAIR), range(KVH), range(N_LANE)
    at = lambda c, d, e, f: (c * N_PAIR + d) * KVH * N_LANE + e * N_LANE + f
    plane = [[at(c, d, e, f) for c in z for e in y] for d in x for f in g]
    line = [[at(c, d, e, f) for d in x for f in g] for c in z for e in y]
    four = [[e * N_LANE + f for f in g] for e in y]
    side = [[at(c, d, e, 2 * f + k) for d in x for f in range(2)] for c in z for e in y for k in range(2)]
    chip = [[2 * f, 2 * f + 1] for f in range(KVH * N_LANE // 2)]
    pairs = [[2 * c, 2 * c + 1] for c in z]
    return plane, line, four, side, chip, pairs


def solution(mesh):
    plane, line, four, side, chip, pairs = groups()
    both = ("hst", "dev")

    def per_device(ctx_query, ctx_key, ctx_value, query, block_lengths, query_positions):
        host = lax.axis_index("hst")
        z, pair = host // N_PAIR, host % N_PAIR
        smem = pl.BlockSpec(memory_space=pltpu.SMEM)
        vmem = pl.BlockSpec(memory_space=pltpu.VMEM)
        hbm = pl.BlockSpec(memory_space=pltpu.HBM)
        params = pltpu.CompilerParams(vmem_limit_bytes=VMEM_LIMIT)
        heavy = pl.CostEstimate(
            flops=800_000_000, bytes_accessed=1_200_000, transcendentals=1 << 20
        )
        dma = pltpu.SemaphoreType.DMA
        shape = lambda dims, dtype: jax.ShapeDtypeStruct(dims, dtype)

        send = pl.pallas_call(
            pack_kernel,
            out_shape=shape((N_Z * KVH, BLK_DEV, 2 * HD), BF),
            in_specs=[hbm, hbm],
            out_specs=hbm,
            scratch_shapes=[
                pltpu.VMEM(ctx_key.shape, BF),
                pltpu.VMEM(ctx_value.shape, BF),
                pltpu.VMEM((KVH, BLK_DEV, 2 * HD), BF),
                dma((2 + N_Z,)),
            ],
        )(ctx_key, ctx_value)
        share = lax.all_to_all(send, both, 0, 0, axis_index_groups=plane)
        share = share.reshape(N_Z * SHARE, 2 * HD)

        couple = lax.all_gather(query, "hst", axis=0, tiled=True, axis_index_groups=pairs)
        seen = lax.all_gather(couple, "dev", axis=0, tiled=True, axis_index_groups=four)
        place = jnp.stack([z, pair, lax.axis_index("dev") % N_LANE, jnp.zeros_like(z)])
        spans = N_PAIR * QN_DEV
        ask, spot, limits, own_spot, gate = pl.pallas_call(
            prep_kernel,
            out_shape=(
                shape((N_PAIR, 2 * N_LANE * QN_DEV, HD), BF),
                shape((8, N_Z * SHARE), F32),
                shape((spans, spans), F32),
                shape((8, ROWS), F32),
                shape((8, HD), F32),
            ),
            in_specs=[vmem, vmem, smem, smem],
            out_specs=(vmem,) * 5,
            compiler_params=params,
        )(seen, query_positions.reshape(N_Z, spans), block_lengths, place)

        share, ask, spot, limits, own_spot, gate = lax.optimization_barrier(
            (share, ask, spot, limits, own_spot, gate)
        )
        local = lax.dynamic_slice_in_dim(share, z * SHARE, SHARE, 0)
        mine = jnp.concatenate([local, share[:SHARE]], axis=0)
        hosts, lanes = range(N_Z * N_PAIR), range(KVH * N_LANE)
        first = share[:SHARE]
        flip = lax.ppermute(mine, "dev", [(i, i ^ 2) for i in lanes])

        dests = N_PAIR * N_LANE
        piece = (dests, QN_DEV + STAT, 2 * HD)
        partial = pl.pallas_call(
            far_kernel,
            out_shape=shape(piece, BF),
            in_specs=[vmem, vmem, vmem, vmem],
            out_specs=hbm,
            scratch_shapes=[pltpu.VMEM(piece, BF), dma((dests,))],
            compiler_params=params,
            cost_estimate=heavy,
        )(ask, share, spot, limits)
        partial, anchor = lax.optimization_barrier((partial, first))
        cross = lax.ppermute(anchor, "hst", [(i, i + 1) for i in hosts if i % 2 == 0])
        skew = lax.ppermute(
            anchor, both,
            [(i * len(lanes) + j, (i + 1) * len(lanes) + (j ^ 2)) for i in hosts if i % 2 == 0 for j in lanes],
        )
        flip, cross, skew = lax.optimization_barrier((flip, cross, skew))
        near_anchor = jnp.where(pair == 0, first, cross)
        far_anchor = jnp.where(pair == 0, flip[SHARE:], skew)
        even = lax.axis_index("dev") % N_LANE < 2
        other = flip[:SHARE]
        near = lax.all_gather(
            jnp.concatenate(
                [
                    jnp.where(even, local, other),
                    jnp.where(even, other, local),
                    near_anchor,
                    far_anchor,
                ],
                axis=0,
            ),
            "dev", axis=0, tiled=True, axis_index_groups=chip,
        )
        arrived = lax.all_to_all(partial, both, 0, 0, axis_index_groups=line)

        ctx_out = pl.pallas_call(
            ctx_kernel,
            out_shape=shape(ctx_query.shape, BF),
            in_specs=[vmem] * 4,
            out_specs=hbm,
            scratch_shapes=[
                pltpu.VMEM(ctx_query.shape, BF),
                pltpu.VMEM((ROWS, 2 * HD), BF),
                dma((ROWS // CTX_ROWS,)),
            ],
            compiler_params=params,
            cost_estimate=heavy,
        )(ctx_query, near, own_spot, gate)
        query_out = pl.pallas_call(
            merge_kernel,
            out_shape=shape(query.shape, BF),
            in_specs=[vmem],
            out_specs=vmem,
            compiler_params=params,
        )(arrived)
        return ctx_out, query_out

    return jax.shard_map(
        per_device,
        mesh=mesh,
        in_specs=(
            P("hst", "dev"),
            P(("hst", "dev"), None),
            P(("hst", "dev"), None),
            P("hst", "dev"),
            P(),
            P(),
        ),
        out_specs=(P("hst", "dev"), P("hst", "dev")),
        check_vma=False,
    )
```

```python
import math

import jax
import jax.numpy as jnp
from jax import lax
from jax.experimental import pallas as pl
from jax.experimental.pallas import tpu as pltpu
from jax.sharding import PartitionSpec as P

H = 64
KVH = 8
HD = 128
N_Z = 8
N_PAIR = 2
N_LANE = 4
BLK_DEV = 16
QN_DEV = 64
ROWS = 512
SHARE = KVH * BLK_DEV
STAT = 16

FAR_BLOCKS = ((0, 0, 256), (0, 256, 256), (1, 0, 256), (1, 256, 128), (1, 384, 128))
CTX_ROWS = 128
NEG = -1e30
FAR = 1 << 20
SCALE2 = HD ** (-0.5) * math.log2(math.e)
BF = jnp.bfloat16
F32 = jnp.float32
NT = (((1,), (1,)), ((), ()))
VMEM_LIMIT = 48 * 1024 * 1024


def pack_kernel(key_hbm, value_hbm, out_hbm, key_ref, value_ref, out_ref, sems):
    fetch = [
        pltpu.make_async_copy(key_hbm, key_ref, sems.at[0]),
        pltpu.make_async_copy(value_hbm, value_ref, sems.at[1]),
    ]
    for copy in fetch:
        copy.start()
    for copy in fetch:
        copy.wait()
    for head in range(KVH):
        cols = slice(head * HD, (head + 1) * HD)
        out_ref[head] = jnp.concatenate([key_ref[:, cols], value_ref[:, cols]], axis=1)
    store = [
        pltpu.make_async_copy(out_ref, out_hbm.at[pl.ds(z * KVH, KVH)], sems.at[2 + z])
        for z in range(N_Z)
    ]
    for copy in store:
        copy.start()
    for copy in store:
        copy.wait()


def with_ones(values):
    return jnp.concatenate([values, jnp.ones_like(values)], axis=1)


def prep_kernel(seen_ref, pos_ref, len_ref, place_ref, q_ref, spot_ref, lim_ref, own_ref, gate_ref):
    z = place_ref[0]
    pair = place_ref[1]
    lane = place_ref[2]
    here = z * N_PAIR + pair
    col = lax.broadcasted_iota(jnp.int32, own_ref.shape, 1)
    own_ref[...] = jnp.where(col < len_ref[here], col, FAR).astype(F32)
    gate_ref[...] = jnp.full(gate_ref.shape, jnp.where(here == 0, -NEG, 0.0), F32)
    for g in range(N_LANE):
        for p in range(N_PAIR):
            at = (g * N_PAIR + p) * QN_DEV
            for h in range(2):
                rows = slice((2 * g + h) * QN_DEV, (2 * g + h + 1) * QN_DEV)
                q_ref[p, rows] = seen_ref[at:at + QN_DEV, h * HD:(h + 1) * HD]
    n = lax.broadcasted_iota(jnp.int32, spot_ref.shape, 1)
    host = (n // SHARE) * N_PAIR + pair
    inner = ((n % SHARE) // BLK_DEV * N_LANE + lane) * BLK_DEV + n % BLK_DEV
    length = jnp.zeros(spot_ref.shape, jnp.int32)
    for h in range(N_Z):
        length = jnp.where(n // SHARE == h, len_ref[h * N_PAIR + pair], length)
    spot_ref[...] = jnp.where(inner < length, host * ROWS + inner, FAR).astype(F32)
    lim_ref[...] = jnp.broadcast_to(pos_ref[pl.ds(z, 1), :].astype(F32), (HD, HD)).T


def far_kernel(q_ref, kv_ref, spot_ref, lim_ref, out_hbm, out_ref, sems):
    count = kv_ref.shape[0]
    spot = spot_ref[0:1, :]
    keys = kv_ref[:, :HD]
    values = with_ones(kv_ref[:, HD:])
    blocks = FAR_BLOCKS
    stores = []

    def score(block):
        p, r, size = block
        return lax.dot_general(
            q_ref[p, r:r + size], keys, NT, preferred_element_type=F32
        )

    def finish(block, s):
        p, r, size = block
        per = size // QN_DEV
        lim = lim_ref[p * QN_DEV:(p + 1) * QN_DEV, :]
        lim = jnp.concatenate([jnp.concatenate([lim] * per, axis=0)] * (count // HD), axis=1)
        s = jnp.where(spot < lim, s, NEG)
        top = jnp.max(s, axis=1, keepdims=True)
        w = jnp.exp2((s - top) * SCALE2).astype(BF)
        mixed = jnp.dot(w, values, preferred_element_type=F32)
        total = mixed[:, HD:]
        level = top * SCALE2 + jnp.log2(total)
        mean = (mixed[:, :HD] / total).astype(BF)
        first = p * N_LANE + r // (2 * QN_DEV)
        for j in range(per // 2):
            d = first + j
            base = j * 2 * QN_DEV
            out_ref[d, :QN_DEV, :HD] = mean[base:base + QN_DEV]
            out_ref[d, :QN_DEV, HD:] = mean[base + QN_DEV:base + 2 * QN_DEV]
            flat = level[base:base + 2 * QN_DEV].T[:STAT]
            high = flat.astype(BF).astype(F32)
            rest = flat - high
            mid = rest.astype(BF).astype(F32)
            row = lax.broadcasted_iota(jnp.int32, (STAT, HD), 0)
            stat = jnp.where(row == 0, high, jnp.where(row == 1, mid, rest - mid))
            out_ref[d, QN_DEV:, :HD] = stat.astype(BF)
            out_ref[d, QN_DEV:, HD:] = jnp.zeros((STAT, HD), BF)
        part = pl.ds(first, per // 2)
        copy = pltpu.make_async_copy(out_ref.at[part], out_hbm.at[part], sems.at[len(stores)])
        copy.start()
        stores.append(copy)

    ahead = score(blocks[0])
    for k, block in enumerate(blocks):
        s = ahead
        if k + 1 < len(blocks):
            ahead = score(blocks[k + 1])
        finish(block, s)
    for copy in stores:
        copy.wait()


def merge_kernel(in_ref, out_ref):
    parts = in_ref.shape[0]
    levels = []
    for k in range(parts):
        stat = in_ref[k, QN_DEV:, :HD].astype(F32)
        levels.append(stat[0:1] + stat[1:2] + stat[2:3])
    level = jnp.concatenate(levels, axis=0)
    w = jnp.exp2(level - jnp.max(level, axis=0, keepdims=True))
    w = w / jnp.sum(w, axis=0, keepdims=True)
    w = jnp.concatenate([w, jnp.zeros((HD - parts, HD), F32)], axis=0).T
    for h in range(2):
        mixed = jnp.zeros((QN_DEV, HD), F32)
        for k in range(parts):
            column = w[h * QN_DEV:(h + 1) * QN_DEV, k:k + 1]
            mixed += column * in_ref[k, :QN_DEV, h * HD:(h + 1) * HD].astype(F32)
        out_ref[:, h * HD:(h + 1) * HD] = mixed.astype(BF)


def ctx_kernel(q_ref, kv_ref, own_ref, gate_ref, ctx_hbm, ctx_ref, local_ref, sems):
    gate = gate_ref[0:1, 0:1]
    stores = []
    for y in range(KVH):
        for g in range(N_LANE):
            to = (y * N_LANE + g) * BLK_DEV
            at = (g % 2 * 4 + g // 2) * SHARE + y * BLK_DEV
            local_ref[to:to + BLK_DEV, :] = kv_ref[at:at + BLK_DEV, :]
    anchor = jnp.concatenate(
        [kv_ref[(4 * c + 2) * SHARE:(4 * c + 4) * SHARE, :] for c in range(2)], axis=0
    )
    anchor_key, anchor_value = anchor[:, :HD], with_ones(anchor[:, HD:])
    step = CTX_ROWS
    spot = own_ref[0:1, :]

    def score(i):
        rows = slice(i * step, (i + 1) * step)
        q = jnp.concatenate([q_ref[rows, :HD], q_ref[rows, HD:]], axis=0)
        a = lax.dot_general(q, anchor_key, NT, preferred_element_type=F32)
        b = lax.dot_general(q, local_ref[:(i + 1) * step, :HD], NT, preferred_element_type=F32)
        return a, b

    def finish(i, a, b):
        n = (i + 1) * step
        rows = slice(i * step, n)
        row = (lax.broadcasted_iota(jnp.int32, (2 * step, n), 0) % step + i * step).astype(F32)
        b = jnp.where(spot[:, :n] <= row, b, NEG)
        top_a = jnp.max(a, axis=1, keepdims=True)
        top = jnp.maximum(top_a - gate, jnp.max(b, axis=1, keepdims=True))
        a = jnp.exp2((a - (top + gate)) * SCALE2).astype(BF)
        b = jnp.exp2((b - top) * SCALE2).astype(BF)
        mixed = jnp.dot(a, anchor_value, preferred_element_type=F32)
        mixed += jnp.dot(b, with_ones(local_ref[:n, HD:]), preferred_element_type=F32)
        mean = (mixed[:, :HD] / mixed[:, HD:]).astype(BF)
        ctx_ref[rows, :HD] = mean[:step]
        ctx_ref[rows, HD:] = mean[step:]
        part = pl.ds(i * step, step)
        copy = pltpu.make_async_copy(ctx_ref.at[part], ctx_hbm.at[part], sems.at[i])
        copy.start()
        stores.append(copy)

    count = ROWS // step
    ahead = score(count - 1)
    for i in reversed(range(count)):
        a, b = ahead
        if i > 0:
            ahead = score(i - 1)
        finish(i, a, b)
    for copy in stores:
        copy.wait()


def groups():
    z, x, y, g = range(N_Z), range(N_PAIR), range(KVH), range(N_LANE)
    at = lambda c, d, e, f: (c * N_PAIR + d) * KVH * N_LANE + e * N_LANE + f
    plane = [[at(c, d, e, f) for c in z for e in y] for d in x for f in g]
    line = [[at(c, d, e, f) for d in x for f in g] for c in z for e in y]
    four = [[e * N_LANE + f for f in g] for e in y]
    side = [[at(c, d, e, 2 * f + k) for d in x for f in range(2)] for c in z for e in y for k in range(2)]
    chip = [[2 * f, 2 * f + 1] for f in range(KVH * N_LANE // 2)]
    pairs = [[2 * c, 2 * c + 1] for c in z]
    return plane, line, four, side, chip, pairs


def solution(mesh):
    plane, line, four, side, chip, pairs = groups()
    both = ("hst", "dev")

    def per_device(ctx_query, ctx_key, ctx_value, query, block_lengths, query_positions):
        host = lax.axis_index("hst")
        z, pair = host // N_PAIR, host % N_PAIR
        smem = pl.BlockSpec(memory_space=pltpu.SMEM)
        vmem = pl.BlockSpec(memory_space=pltpu.VMEM)
        hbm = pl.BlockSpec(memory_space=pltpu.HBM)
        params = pltpu.CompilerParams(vmem_limit_bytes=VMEM_LIMIT)
        heavy = pl.CostEstimate(
            flops=800_000_000, bytes_accessed=1_200_000, transcendentals=1 << 20
        )
        dma = pltpu.SemaphoreType.DMA
        shape = lambda dims, dtype: jax.ShapeDtypeStruct(dims, dtype)

        send = pl.pallas_call(
            pack_kernel,
            out_shape=shape((N_Z * KVH, BLK_DEV, 2 * HD), BF),
            in_specs=[hbm, hbm],
            out_specs=hbm,
            scratch_shapes=[
                pltpu.VMEM(ctx_key.shape, BF),
                pltpu.VMEM(ctx_value.shape, BF),
                pltpu.VMEM((KVH, BLK_DEV, 2 * HD), BF),
                dma((2 + N_Z,)),
            ],
        )(ctx_key, ctx_value)
        share = lax.all_to_all(send, both, 0, 0, axis_index_groups=plane)
        share = share.reshape(N_Z * SHARE, 2 * HD)

        couple = lax.all_gather(query, "hst", axis=0, tiled=True, axis_index_groups=pairs)
        seen = lax.all_gather(couple, "dev", axis=0, tiled=True, axis_index_groups=four)
        place = jnp.stack([z, pair, lax.axis_index("dev") % N_LANE, jnp.zeros_like(z)])
        spans = N_PAIR * QN_DEV
        ask, spot, limits, own_spot, gate = pl.pallas_call(
            prep_kernel,
            out_shape=(
                shape((N_PAIR, 2 * N_LANE * QN_DEV, HD), BF),
                shape((8, N_Z * SHARE), F32),
                shape((spans, spans), F32),
                shape((8, ROWS), F32),
                shape((8, HD), F32),
            ),
            in_specs=[vmem, vmem, smem, smem],
            out_specs=(vmem,) * 5,
            compiler_params=params,
        )(seen, query_positions.reshape(N_Z, spans), block_lengths, place)

        share, ask, spot, limits, own_spot, gate = lax.optimization_barrier(
            (share, ask, spot, limits, own_spot, gate)
        )
        local = lax.dynamic_slice_in_dim(share, z * SHARE, SHARE, 0)
        mine = jnp.concatenate([local, share[:SHARE]], axis=0)
        hosts, lanes = range(N_Z * N_PAIR), range(KVH * N_LANE)
        first = share[:SHARE]
        flip = lax.ppermute(mine, "dev", [(i, i ^ 2) for i in lanes])

        dests = N_PAIR * N_LANE
        piece = (dests, QN_DEV + STAT, 2 * HD)
        partial = pl.pallas_call(
            far_kernel,
            out_shape=shape(piece, BF),
            in_specs=[vmem, vmem, vmem, vmem],
            out_specs=hbm,
            scratch_shapes=[pltpu.VMEM(piece, BF), dma((dests,))],
            compiler_params=params,
            cost_estimate=heavy,
        )(ask, share, spot, limits)
        partial, anchor = lax.optimization_barrier((partial, first))
        cross = lax.ppermute(anchor, "hst", [(i, i + 1) for i in hosts if i % 2 == 0])
        skew = lax.ppermute(
            anchor, both,
            [(i * len(lanes) + j, (i + 1) * len(lanes) + (j ^ 2)) for i in hosts if i % 2 == 0 for j in lanes],
        )
        flip, cross, skew = lax.optimization_barrier((flip, cross, skew))
        near_anchor = jnp.where(pair == 0, first, cross)
        far_anchor = jnp.where(pair == 0, flip[SHARE:], skew)
        even = lax.axis_index("dev") % N_LANE < 2
        other = flip[:SHARE]
        near = lax.all_gather(
            jnp.concatenate(
                [
                    jnp.where(even, local, other),
                    jnp.where(even, other, local),
                    near_anchor,
                    far_anchor,
                ],
                axis=0,
            ),
            "dev", axis=0, tiled=True, axis_index_groups=chip,
        )
        arrived = lax.all_to_all(partial, both, 0, 0, axis_index_groups=line)

        ctx_out = pl.pallas_call(
            ctx_kernel,
            out_shape=shape(ctx_query.shape, BF),
            in_specs=[vmem] * 4,
            out_specs=hbm,
            scratch_shapes=[
                pltpu.VMEM(ctx_query.shape, BF),
                pltpu.VMEM((ROWS, 2 * HD), BF),
                dma((ROWS // CTX_ROWS,)),
            ],
            compiler_params=params,
            cost_estimate=heavy,
        )(ctx_query, near, own_spot, gate)
        query_out = pl.pallas_call(
            merge_kernel,
            out_shape=shape(query.shape, BF),
            in_specs=[vmem],
            out_specs=vmem,
            compiler_params=params,
        )(arrived)
        return ctx_out, query_out

    return jax.shard_map(
        per_device,
        mesh=mesh,
        in_specs=(
            P("hst", "dev"),
            P(("hst", "dev"), None),
            P(("hst", "dev"), None),
            P("hst", "dev"),
            P(),
            P(),
        ),
        out_specs=(P("hst", "dev"), P("hst", "dev")),
        check_vma=False,
    )
```
